256 devices in a mesh: pw: 32 (over z_lo, y, core), band: 8 (over x, z_hi).
Axes of the slice: x: 4, y: 4, z: 8 (z_hi: 2, z_lo: 4; z = z_hi * 4 + z_lo), core: 2. Of those that a mesh axis runs over, the one named last changes fastest.
Arguments:
- waves: bfloat16 [2, 40960, 7168], P(None, 'pw', 'band'), may hold values from -6 to 6
- projectors: bfloat16 [2, 128, 40960], P(None, 'band', 'pw'), may hold values from -0.01953125 to 0.01953125
- coupling: float32 [12, 13, 13], replicated, may hold values from -32.19938 to 32.19938
- offsets: int32 [12], replicated, may hold values from 0 to 119, as said below
- counts: int32 [12], replicated, may hold values from 9 to 13, as said below
Outputs:
- applied: bfloat16 [2, 40960, 7168], P(None, 'pw', 'band')
The draws below stay inside these ranges and needn't reach their ends.
Inputs may be any that keep to these rules, and one draw needn't show every extreme that they name: `counts`: each atom has 9 or 13 projectors, exactly 5 atoms have 13, so the atoms fill all 128 projectors. offsets are the running sums of counts before each atom, so atoms take consecutive projectors in order.
All inputs are finite; a program needn't handle non-finite values.
Results may differ from the reference program's by a relative error of at most 0.0049.
Values may be sent and summed in bfloat16 or wider, within the bound.
No kernel may reach another device: no remote copies, remote signals or barrier semaphores. Data moves between devices by JAX's collectives and lax.ppermute only.
A program may use at most 64 MiB of HBM per device.

```python
import jax
import jax.numpy as jnp
from jax import lax

NB_DEV = 896
NP = 128
NATOM = 12
M = 13
NPW = 40960
NB = 7168
N_BAND = 8


def atom_sizes(key):
    order = jax.random.permutation(key, NATOM)
    return jnp.where(order < 5, 13, 9).astype(jnp.int32)


def draw_counts(key, part):
    return atom_sizes(key)


def draw_offsets(key, part):
    sizes = atom_sizes(key)
    return (jnp.cumsum(sizes) - sizes).astype(jnp.int32)


def steps_of(key, extent, cuts, low, largest):
    def one(position, parts):
        steps = jax.random.uniform(jax.random.fold_in(jax.random.fold_in(key, 6), position), (parts,), jnp.float32, low / len(cuts), largest / len(cuts))
        return jnp.repeat(jnp.exp(steps), extent[position] // parts).reshape((-1,) + (1,) * (len(extent) - position - 1))

    level = one(*cuts[0])
    for cut in cuts[1:]:
        level = level * one(*cut)
    return level


def scatter_about(key, extent, scale, reach, shards=(), held_as=jnp.bfloat16):
    array = jax.random.normal(key, extent, jnp.float32) * scale
    if len(shards) > 0:
        array = steps_of(key, extent, shards, -0.22, 0.18) * array
    return jnp.clip(array, min=-reach, max=reach).astype(held_as)


def setup_inputs(seed: int = 0) -> dict:
    key_list = jax.random.split(jax.random.key(seed), 6)
    return {
        "waves": scatter_about(key_list[0], (2, NPW, NB), 1.0, 6.0, ((1, 32), (2, 8))),
        "projectors": scatter_about(key_list[1], (2, NP, NPW), (2 * NPW) ** -0.5, 0.01953125, ((1, 8), (2, 32))),
        "coupling": scatter_about(key_list[2], (NATOM, M, M), (0.3 * (NPW / NP) ** 0.5), 32.19938, (), jnp.float32),
        "offsets": draw_offsets(jax.random.fold_in(key_list[5], 71), 0),
        "counts": draw_counts(jax.random.fold_in(key_list[5], 71), 0),
    }


def coupling_block(coupling, offsets, counts):
    proj = jnp.arange(NP, dtype=jnp.int32)
    local = jnp.arange(M, dtype=jnp.int32)
    target = offsets[:, None] + local[None, :]
    select = (proj[None, :, None] == target[:, None, :]) & (local[None, None, :] < counts[:, None, None])
    select = select.astype(jnp.float32)
    sym = (coupling + jnp.swapaxes(coupling, 1, 2)) * 0.5
    return jnp.einsum('api,aij,aqj->pq', select, sym, select, precision=lax.Precision.HIGHEST)


def reference(waves, projectors, coupling, offsets, counts):
    block = coupling_block(coupling, offsets, counts)

    def one_block(index):
        start = (index * NB_DEV).astype(jnp.int32)
        part = lax.dynamic_slice_in_dim(waves, start, NB_DEV, 2)
        real = jnp.dot(projectors[0], part[0], preferred_element_type=jnp.float32) + jnp.dot(projectors[1], part[1], preferred_element_type=jnp.float32)
        imag = jnp.dot(projectors[0], part[1], preferred_element_type=jnp.float32) - jnp.dot(projectors[1], part[0], preferred_element_type=jnp.float32)
        coeffs = jnp.stack([real, imag])
        coupled = jnp.einsum('pq,kqb->kpb', block, coeffs, precision=lax.Precision.HIGHEST).astype(jnp.bfloat16)
        dims = (((0,), (0,)), ((), ()))
        out_real = lax.dot_general(projectors[0], coupled[0], dims, preferred_element_type=jnp.float32) - lax.dot_general(projectors[1], coupled[1], dims, preferred_element_type=jnp.float32)
        out_imag = lax.dot_general(projectors[0], coupled[1], dims, preferred_element_type=jnp.float32) + lax.dot_general(projectors[1], coupled[0], dims, preferred_element_type=jnp.float32)
        return jnp.stack([out_real, out_imag]).astype(jnp.bfloat16)

    blocks = lax.map(one_block, jnp.arange(N_BAND, dtype=jnp.int32))
    return jnp.transpose(blocks, (1, 2, 0, 3)).reshape(2, NPW, NB)
```

```python
import jax
import jax.numpy as jnp
from jax import lax
from jax.experimental import pallas as pl
from jax.experimental.pallas import tpu as pltpu
from jax.sharding import PartitionSpec as P

NP = 128
M = 13
ROWS = 16
NPW_DEV = 1280
NB_DEV = 896
CHUNK = 32
BLOCK_PW = 256
BF16 = jnp.bfloat16
F32 = jnp.float32


def coupling_block(coupling, offsets, counts, proj):
    local = jnp.arange(M, dtype=jnp.int32)
    target = offsets[:, None] + local[None, :]
    select = (proj[None, :, None] == target[:, None, :]) & (
        local[None, None, :] < counts[:, None, None]
    )
    select = select.astype(jnp.float32)
    sym = (coupling + jnp.swapaxes(coupling, 1, 2)) * 0.5
    return jnp.einsum("api,aij,aqj->pq", select, sym, select, precision=lax.Precision.HIGHEST)


def over_pw(x, bits):
    return lax.ppermute(x, "pw", [(i, i ^ bits) for i in range(32)])


def over_band(x, bits):
    return lax.ppermute(x, "band", [(i, i ^ bits) for i in range(8)])


def two_terms(x):
    high = x.astype(BF16)
    return high, (x - high.astype(F32)).astype(BF16)


def project_kernel(place_ref, block_ref, *refs):
    pieces, (waves_ref, keep_ref, send_ref, rows_ref) = refs[:8], refs[8:]
    core, y = place_ref[0], place_ref[1]
    for r, piece in enumerate(pieces):
        for k in range(2):
            rows_ref[pl.ds(k * NP + r * ROWS, ROWS), :] = piece[k]
    rows = rows_ref[...]
    first = jnp.dot(rows, waves_ref[0], preferred_element_type=F32)
    second = jnp.dot(rows, waves_ref[1], preferred_element_type=F32)
    real = first[:NP] + second[NP:]
    imag = second[:NP] - first[NP:]
    block_high, block_low = two_terms(block_ref[...])
    left = jnp.concatenate([block_high, block_high, block_low], axis=1)

    def couple(part):
        high, low = two_terms(part)
        right = jnp.concatenate([high, low, high], axis=0)
        return jnp.dot(left, right, preferred_element_type=F32)

    real, imag = couple(real), couple(imag)
    keep = jnp.where(core == 0, real, imag)
    send = jnp.where(core == 0, imag, real)
    for t in range(4):
        at = jnp.bitwise_xor(y, t)
        keep_ref[at] = keep[t * CHUNK : (t + 1) * CHUNK]
        send_ref[at] = send[t * CHUNK : (t + 1) * CHUNK]


def project(place, block, pieces, waves):
    vmem = pl.BlockSpec(memory_space=pltpu.VMEM)
    half = jax.ShapeDtypeStruct((4, CHUNK, NB_DEV), F32)
    return pl.pallas_call(
        project_kernel,
        out_shape=(half, half),
        in_specs=[pl.BlockSpec(memory_space=pltpu.SMEM)] + [vmem] * 10,
        out_specs=(vmem, vmem),
        scratch_shapes=[pltpu.VMEM((2 * NP, NPW_DEV), BF16)],
        compiler_params=pltpu.CompilerParams(vmem_limit_bytes=24 * 1024 * 1024),
        cost_estimate=pl.CostEstimate(
            flops=4 * 2 * NP * NPW_DEV * NB_DEV, bytes_accessed=6 * 1024 * 1024, transcendentals=0
        ),
    )(place, block, *pieces, waves)


def turn_kernel(*refs):
    pieces, out_ref, rows_ref = refs[:8], refs[8], refs[9]
    for r, piece in enumerate(pieces):
        for k in range(2):
            rows_ref[pl.ds(k * NP + r * ROWS, ROWS), :] = piece[k]
    out_ref[...] = rows_ref[...].T


def turn(pieces):
    vmem = pl.BlockSpec(memory_space=pltpu.VMEM)
    return pl.pallas_call(
        turn_kernel,
        out_shape=jax.ShapeDtypeStruct((NPW_DEV, 2 * NP), BF16),
        in_specs=[vmem] * 8,
        out_specs=vmem,
        scratch_shapes=[pltpu.VMEM((2 * NP, NPW_DEV), BF16)],
        compiler_params=pltpu.CompilerParams(vmem_limit_bytes=16 * 1024 * 1024),
        cost_estimate=pl.CostEstimate(
            flops=2 * NP * NPW_DEV, bytes_accessed=4 * 1024 * 1024, transcendentals=0
        ),
    )(*pieces)


def spread_kernel(place_ref, own_ref, other_ref, turned_ref, out_ref, right_ref):
    @pl.when(pl.program_id(0) == 0)
    def _():
        core, y = place_ref[0], place_ref[1]
        for t in range(4):
            at = jnp.bitwise_xor(y, t)
            own, other = own_ref[at], other_ref[at]
            real = jnp.where(core == 0, own, other)
            imag = jnp.where(core == 0, other, own)
            low, high = pl.ds(t * CHUNK, CHUNK), pl.ds(NP + t * CHUNK, CHUNK)
            right_ref[0, low, :] = real
            right_ref[0, high, :] = -imag
            right_ref[1, low, :] = imag
            right_ref[1, high, :] = real

    left = turned_ref[...]
    for k in range(2):
        out_ref[k] = jnp.dot(left, right_ref[k], preferred_element_type=F32).astype(BF16)


def spread_back(place, own, other, turned):
    whole = pl.BlockSpec((4, CHUNK, NB_DEV), lambda i: (0, 0, 0))
    return pl.pallas_call(
        spread_kernel,
        grid=(NPW_DEV // BLOCK_PW,),
        out_shape=jax.ShapeDtypeStruct((2, NPW_DEV, NB_DEV), BF16),
        in_specs=[
            pl.BlockSpec(memory_space=pltpu.SMEM),
            whole,
            whole,
            pl.BlockSpec((BLOCK_PW, 2 * NP), lambda i: (i, 0)),
        ],
        out_specs=pl.BlockSpec((2, BLOCK_PW, NB_DEV), lambda i: (0, i, 0)),
        scratch_shapes=[pltpu.VMEM((2, 2 * NP, NB_DEV), BF16)],
        compiler_params=pltpu.CompilerParams(vmem_limit_bytes=16 * 1024 * 1024),
        cost_estimate=pl.CostEstimate(
            flops=4 * 2 * NP * NPW_DEV * NB_DEV, bytes_accessed=6 * 1024 * 1024, transcendentals=0
        ),
    )(place, own, other, turned)


def shards(waves, projectors, coupling, offsets, counts):
    pw, band = lax.axis_index("pw"), lax.axis_index("band")
    core, y = pw & 1, (pw >> 1) & 3
    place = jnp.stack([core, y])

    far = over_band(projectors, 1)
    near = [over_band(projectors, bits) for bits in (2, 6, 4)]
    rest = [over_band(far, bits) for bits in (2, 6, 4)]
    pieces = [projectors, far, near[0], rest[0], near[2], rest[2], near[1], rest[1]]
    proj = jnp.arange(NP, dtype=jnp.int32) ^ (band * ROWS)
    block = coupling_block(coupling, offsets, counts, proj)

    keep, send = project(place, block, pieces, waves)
    turned = turn(pieces)
    total = keep + over_pw(send, 1)

    sums = total[0]
    for arrived in [over_pw(total[s].astype(BF16), 2 * s) for s in (1, 3, 2)]:
        sums = sums + arrived.astype(F32)
    sent = sums.astype(BF16)
    for arrived in [over_pw(sent, 8 * s) for s in (1, 2, 3)]:
        sums = sums + arrived.astype(F32)
    mine = sums.astype(BF16)
    chunk = {s: over_pw(mine, 2 * s) for s in (1, 3, 2)}
    own = jnp.stack([mine, chunk[1], chunk[2], chunk[3]])
    other = over_pw(own, 1)
    return spread_back(place, own, other, turned)


def solution(mesh):
    placed = (P(None, "pw", "band"), P(None, "band", "pw"), P(), P(), P())
    return jax.shard_map(
        shards, mesh=mesh, in_specs=placed, out_specs=P(None, "pw", "band"), check_vma=False
    )
```

```python
import jax
import jax.numpy as jnp
from jax import lax
from jax.experimental import pallas as pl
from jax.experimental.pallas import tpu as pltpu
from jax.sharding import PartitionSpec as P

NP = 128
NATOM = 12
M = 13
ROWS = 16
HALF = 64
NPW_DEV = 1280
NB_DEV = 896
CHUNK = 32
BLOCK_PW = 640
BF16 = jnp.bfloat16
F32 = jnp.float32
MIB = 1024 * 1024


def over_pw(x, bits):
    return lax.ppermute(x, "pw", [(i, i ^ bits) for i in range(32)])


def over_band(x, bits):
    return lax.ppermute(x, "band", [(i, i ^ bits) for i in range(8)])


def vmem():
    return pl.BlockSpec(memory_space=pltpu.VMEM)


def smem():
    return pl.BlockSpec(memory_space=pltpu.SMEM)


def params(mib):
    return pltpu.CompilerParams(vmem_limit_bytes=mib * MIB)


def cost(flops, nbytes):
    return pl.CostEstimate(flops=flops, bytes_accessed=nbytes, transcendentals=0)


def two_terms(x):
    high = x.astype(BF16)
    return high, (x - high.astype(F32)).astype(BF16)


def ahead_kernel(
    pick_ref,
    offsets_hbm,
    counts_hbm,
    coupling_hbm,
    waves_hbm,
    left_ref,
    waves_ref,
    placed_ref,
    offsets_ref,
    counts_ref,
    coupling_ref,
    sem,
):
    pairs = (
        (offsets_hbm, offsets_ref),
        (counts_hbm, counts_ref),
        (coupling_hbm, coupling_ref),
        (waves_hbm, waves_ref),
    )
    copies = [pltpu.make_async_copy(a, b, sem.at[i]) for i, (a, b) in enumerate(pairs)]
    for copy in copies:
        copy.start()
    placed_ref[...] = jnp.zeros(placed_ref.shape, F32)
    for copy in copies[:3]:
        copy.wait()
    row = lax.broadcasted_iota(jnp.int32, (M, NP), 0)
    column = lax.broadcasted_iota(jnp.int32, (M, NP), 1)
    for atom in range(NATOM):
        at, count = offsets_ref[atom], counts_ref[atom]
        wide = jnp.concatenate([coupling_ref[atom], jnp.zeros((M, NP - M), F32)], axis=1)
        wide = jnp.where((row < count) & (column < count), wide, 0.0)
        placed_ref[pl.ds(at, M), :] = pltpu.roll(wide, at, 1)
    placed = placed_ref[:NP, :]
    block = (placed + placed.T) * 0.5
    pick, pick_turned = pick_ref[0], pick_ref[1]

    def reorder(part):
        part = jnp.dot(part, pick, preferred_element_type=F32).astype(BF16)
        return jnp.dot(pick_turned, part, preferred_element_type=F32).astype(BF16)

    high, low = (reorder(part) for part in two_terms(block))
    left_ref[...] = jnp.concatenate([high, high, low], axis=1)
    copies[3].wait()


def pick_kernel(band_ref, pick_ref):
    place = lax.broadcasted_iota(jnp.int32, (NP, NP), 1)
    piece = place >> 4
    piece = ((piece & 3) << 1) | (piece >> 2)
    number = (jnp.bitwise_xor(piece, band_ref[0]) << 4) | (place & 15)
    pick = (lax.broadcasted_iota(jnp.int32, (NP, NP), 0) == number).astype(F32)
    pick_ref[0] = pick.astype(BF16)
    pick_ref[1] = pick.T.astype(BF16)


def gathered_order(band):
    return pl.pallas_call(
        pick_kernel,
        out_shape=jax.ShapeDtypeStruct((2, NP, NP), BF16),
        in_specs=[smem()],
        out_specs=vmem(),
        compiler_params=params(8),
        cost_estimate=cost(4 * 10**9, 1),
    )(band)


def ahead(pick, offsets, counts, coupling, waves):
    hbm = pl.BlockSpec(memory_space=pltpu.HBM)
    return pl.pallas_call(
        ahead_kernel,
        out_shape=(
            jax.ShapeDtypeStruct((NP, 3 * NP), BF16),
            jax.ShapeDtypeStruct(waves.shape, BF16),
        ),
        in_specs=[vmem()] + [hbm] * 4,
        out_specs=(vmem(), vmem()),
        scratch_shapes=[
            pltpu.VMEM((NP + ROWS, NP), F32),
            pltpu.SMEM((NATOM,), jnp.int32),
            pltpu.SMEM((NATOM,), jnp.int32),
            pltpu.VMEM((NATOM, M, M), F32),
            pltpu.SemaphoreType.DMA((4,)),
        ],
        compiler_params=params(46),
        cost_estimate=cost(2 * 10**9, 8 * MIB),
    )(pick, offsets, counts, coupling, waves)


def fill_rows(pieces, rows_ref):
    for i, piece in enumerate(pieces):
        at = (i // 4) * HALF + (3 - i % 4) * ROWS
        for k in range(2):
            rows_ref[pl.ds(k * NP + at, ROWS), :] = piece[k]


def project_kernel(place_ref, left_ref, waves_ref, *refs):
    pieces, (keep_ref, send_ref, rows_ref) = refs[:8], refs[8:]
    core, y = place_ref[0], place_ref[1]
    fill_rows(pieces, rows_ref)
    rows = rows_ref[...]
    first = jnp.dot(rows, waves_ref[0], preferred_element_type=F32)
    second = jnp.dot(rows, waves_ref[1], preferred_element_type=F32)
    left = left_ref[...]

    def couple(part):
        high, low = two_terms(part)
        right = jnp.concatenate([high, low, high], axis=0)
        return jnp.dot(left, right, preferred_element_type=F32)

    real = couple(first[:NP] + second[NP:])
    imag = couple(second[:NP] - first[NP:])
    keep = jnp.where(core == 0, real, imag)
    send = jnp.where(core == 0, imag, real)
    for t in range(4):
        at = jnp.bitwise_xor(y, t)
        keep_ref[at] = keep[t * CHUNK : (t + 1) * CHUNK]
        send_ref[at] = send[t * CHUNK : (t + 1) * CHUNK]


def project(place, left, waves, pieces):
    half = jax.ShapeDtypeStruct((4, CHUNK, NB_DEV), F32)
    return pl.pallas_call(
        project_kernel,
        out_shape=(half, half),
        in_specs=[smem()] + [vmem()] * 10,
        out_specs=(vmem(), vmem()),
        scratch_shapes=[pltpu.VMEM((2 * NP, NPW_DEV), BF16)],
        compiler_params=params(16),
        cost_estimate=cost(8 * NP * NPW_DEV * NB_DEV, 6 * MIB),
    )(place, left, waves, *pieces)


def turn_kernel(*refs):
    pieces, (out_ref, rows_ref) = refs[:8], refs[8:]
    fill_rows(pieces, rows_ref)
    turned = rows_ref[...].T
    first, second = turned[:, :NP], turned[:, NP:]
    out_ref[0, :, :NP] = first
    out_ref[0, :, NP:] = -second
    out_ref[1, :, :NP] = second
    out_ref[1, :, NP:] = first


def turn(pieces):
    return pl.pallas_call(
        turn_kernel,
        out_shape=jax.ShapeDtypeStruct((2, NPW_DEV, 2 * NP), BF16),
        in_specs=[vmem()] * 8,
        out_specs=vmem(),
        scratch_shapes=[pltpu.VMEM((2 * NP, NPW_DEV), BF16)],
        compiler_params=params(16),
        cost_estimate=cost(2 * NP * NPW_DEV, 2 * MIB),
    )(*pieces)


def spread_kernel(place_ref, own_ref, other_ref, turned_ref, out_ref, right_ref, result_ref, sem):
    core, y = place_ref[0], place_ref[1]
    for s in range(4):
        at = jnp.bitwise_xor(y, s) * CHUNK
        own_at = pl.multiple_of(core * NP + at, CHUNK)
        other_at = pl.multiple_of((1 - core) * NP + at, CHUNK)
        right_ref[pl.ds(own_at, CHUNK), :] = own_ref[s]
        right_ref[pl.ds(other_at, CHUNK), :] = other_ref[s]
    right = right_ref[...]
    copies = []
    for k in range(2):
        for at in range(0, NPW_DEV, BLOCK_PW):
            rows = pl.ds(at, BLOCK_PW)
            result_ref[k, rows, :] = jnp.dot(
                turned_ref[k, rows, :], right, preferred_element_type=F32
            ).astype(BF16)
            copy = pltpu.make_async_copy(
                result_ref.at[k, rows], out_ref.at[k, rows], sem.at[len(copies)]
            )
            copy.start()
            copies.append(copy)
    for copy in copies:
        copy.wait()


def spread_back(place, own, other, turned):
    return pl.pallas_call(
        spread_kernel,
        out_shape=jax.ShapeDtypeStruct((2, NPW_DEV, NB_DEV), BF16),
        in_specs=[smem()] + [vmem()] * 3,
        out_specs=pl.BlockSpec(memory_space=pltpu.HBM),
        scratch_shapes=[
            pltpu.VMEM((2 * NP, NB_DEV), BF16),
            pltpu.VMEM((2, NPW_DEV, NB_DEV), BF16),
            pltpu.SemaphoreType.DMA((2 * NPW_DEV // BLOCK_PW,)),
        ],
        compiler_params=params(16),
        cost_estimate=cost(8 * NP * NPW_DEV * NB_DEV, 6 * MIB),
    )(place, own, other, turned)


def shards(waves, projectors, coupling, offsets, counts):
    pw, band = lax.axis_index("pw"), lax.axis_index("band")
    place = jnp.stack([pw & 1, (pw >> 1) & 3])

    distant = over_band(projectors, 1)
    near = [over_band(projectors, bits) for bits in (6, 4, 2)] + [projectors]
    far = [over_band(distant, bits) for bits in (6, 4, 2)] + [distant]
    pick = gathered_order(band.reshape(1))
    pick, _ = lax.optimization_barrier((pick, distant))
    left, waves = ahead(pick, offsets, counts, coupling, waves)
    keep, send = project(place, left, waves, near + far)
    turned = turn(near + far)
    total = keep + over_pw(send, 1)

    sums = total[0]
    for arrived in [over_pw(total[s].astype(BF16), 2 * s) for s in (3, 2, 1)]:
        sums = sums + arrived.astype(F32)
    sent = sums.astype(BF16)
    for arrived in [over_pw(sent, 8 * s) for s in (3, 2, 1)]:
        sums = sums + arrived.astype(F32)
    mine = sums.astype(BF16)
    chunk = {s: over_pw(mine, 2 * s) for s in (3, 2, 1)}
    own = jnp.stack([mine, chunk[1], chunk[2], chunk[3]])
    other = over_pw(own, 1)
    return spread_back(place, own, other, turned)


def solution(mesh):
    placed = (P(None, "pw", "band"), P(None, "band", "pw"), P(), P(), P())
    return jax.shard_map(
        shards, mesh=mesh, in_specs=placed, out_specs=P(None, "pw", "band"), check_vma=False
    )
```

```python
import jax
import jax.numpy as jnp
from jax import lax
from jax.experimental import pallas as pl
from jax.experimental.pallas import tpu as pltpu
from jax.sharding import PartitionSpec as P

NP = 128
NATOM = 12
M = 13
ROWS = 16
HALF = 64
NPW_DEV = 1280
NB_DEV = 896
CHUNK = 32
BLOCK_PW = 640
BF16 = jnp.bfloat16
F32 = jnp.float32
MIB = 1024 * 1024


def over_pw(x, bits):
    return lax.ppermute(x, "pw", [(i, i ^ bits) for i in range(32)])


def over_band(x, bits):
    return lax.ppermute(x, "band", [(i, i ^ bits) for i in range(8)])


def vmem():
    return pl.BlockSpec(memory_space=pltpu.VMEM)


def smem():
    return pl.BlockSpec(memory_space=pltpu.SMEM)


def params(mib):
    return pltpu.CompilerParams(vmem_limit_bytes=mib * MIB)


def cost(flops, nbytes):
    return pl.CostEstimate(flops=flops, bytes_accessed=nbytes, transcendentals=0)


def two_terms(x):
    high = x.astype(BF16)
    return high, (x - high.astype(F32)).astype(BF16)


def ahead_kernel(
    pick_ref,
    offsets_hbm,
    counts_hbm,
    coupling_hbm,
    waves_hbm,
    left_ref,
    waves_ref,
    placed_ref,
    offsets_ref,
    counts_ref,
    coupling_ref,
    sem,
):
    pairs = (
        (offsets_hbm, offsets_ref),
        (counts_hbm, counts_ref),
        (coupling_hbm, coupling_ref),
        (waves_hbm, waves_ref),
    )
    copies = [pltpu.make_async_copy(a, b, sem.at[i]) for i, (a, b) in enumerate(pairs)]
    for copy in copies:
        copy.start()
    placed_ref[...] = jnp.zeros(placed_ref.shape, F32)
    for copy in copies[:3]:
        copy.wait()
    row = lax.broadcasted_iota(jnp.int32, (M, NP), 0)
    column = lax.broadcasted_iota(jnp.int32, (M, NP), 1)
    for atom in range(NATOM):
        at, count = offsets_ref[atom], counts_ref[atom]
        wide = jnp.concatenate([coupling_ref[atom], jnp.zeros((M, NP - M), F32)], axis=1)
        wide = jnp.where((row < count) & (column < count), wide, 0.0)
        placed_ref[pl.ds(at, M), :] = pltpu.roll(wide, at, 1)
    placed = placed_ref[:NP, :]
    block = (placed + placed.T) * 0.5
    pick, pick_turned = pick_ref[0], pick_ref[1]

    def reorder(part):
        part = jnp.dot(part, pick, preferred_element_type=F32).astype(BF16)
        return jnp.dot(pick_turned, part, preferred_element_type=F32).astype(BF16)

    high, low = (reorder(part) for part in two_terms(block))
    for h in range(2):
        columns = slice(h * HALF, (h + 1) * HALF)
        left_ref[h] = jnp.concatenate(
            [high[:, columns], high[:, columns], low[:, columns]], axis=1
        )
    copies[3].wait()


def pick_kernel(y_ref, band_ref, pick_ref):
    def pick(place):
        piece = place >> 4
        piece = ((piece & 3) << 1) | (piece >> 2)
        number = (jnp.bitwise_xor(piece, band_ref[0]) << 4) | (place & 15)
        projector = lax.broadcasted_iota(jnp.int32, (NP, NP), 0)
        return (projector == number).astype(F32)

    place = lax.broadcasted_iota(jnp.int32, (NP, NP), 1)
    pick_ref[0] = pick(place).astype(BF16)
    pick_ref[1] = pick(jnp.bitwise_xor(place, y_ref[0] << 5)).T.astype(BF16)


def gathered_order(y, band):
    return pl.pallas_call(
        pick_kernel,
        out_shape=jax.ShapeDtypeStruct((2, NP, NP), BF16),
        in_specs=[smem(), smem()],
        out_specs=vmem(),
        compiler_params=params(8),
        cost_estimate=cost(4 * 10**9, 1),
    )(y, band)


def ahead(pick, offsets, counts, coupling, waves):
    hbm = pl.BlockSpec(memory_space=pltpu.HBM)
    return pl.pallas_call(
        ahead_kernel,
        out_shape=(
            jax.ShapeDtypeStruct((2, NP, 3 * HALF), BF16),
            jax.ShapeDtypeStruct(waves.shape, BF16),
        ),
        in_specs=[vmem()] + [hbm] * 4,
        out_specs=(vmem(), vmem()),
        scratch_shapes=[
            pltpu.VMEM((NP + ROWS, NP), F32),
            pltpu.SMEM((NATOM,), jnp.int32),
            pltpu.SMEM((NATOM,), jnp.int32),
            pltpu.VMEM((NATOM, M, M), F32),
            pltpu.SemaphoreType.DMA((4,)),
        ],
        compiler_params=params(46),
        cost_estimate=cost(2 * 10**9, 8 * MIB),
    )(pick, offsets, counts, coupling, waves)


def coupled_parts(h, pieces, left_ref, waves_ref, rows_ref):
    for i, piece in enumerate(pieces):
        at = (3 - i) * ROWS
        rows_ref[pl.ds(at, ROWS), :] = piece[0]
        rows_ref[pl.ds(HALF + at, ROWS), :] = piece[1]
    rows = rows_ref[...]
    first = jnp.dot(rows, waves_ref[0], preferred_element_type=F32)
    second = jnp.dot(rows, waves_ref[1], preferred_element_type=F32)
    left = left_ref[h]

    def couple(part):
        high, low = two_terms(part)
        right = jnp.concatenate([high, low, high], axis=0)
        return jnp.dot(left, right, preferred_element_type=F32)

    return couple(first[:HALF] + second[HALF:]), couple(second[:HALF] - first[HALF:])


def near_kernel(left_ref, waves_ref, *refs):
    pieces, (out_ref, rows_ref) = refs[:4], refs[4:]
    out_ref[0], out_ref[1] = coupled_parts(0, pieces, left_ref, waves_ref, rows_ref)


def project_near(left, waves, pieces):
    return pl.pallas_call(
        near_kernel,
        out_shape=jax.ShapeDtypeStruct((2, NP, NB_DEV), F32),
        in_specs=[vmem()] * 6,
        out_specs=vmem(),
        scratch_shapes=[pltpu.VMEM((NP, NPW_DEV), BF16)],
        compiler_params=params(16),
        cost_estimate=cost(4 * NP * NPW_DEV * NB_DEV, 6 * MIB),
    )(left, waves, *pieces)


def far_kernel(core_ref, near_ref, left_ref, waves_ref, *refs):
    pieces, (keep_ref, send_ref, rows_ref) = refs[:4], refs[4:]

    def sums(out_refs):
        parts = coupled_parts(1, pieces, left_ref, waves_ref, rows_ref)
        for k in range(2):
            out_refs[k][...] = parts[k] + near_ref[k]

    @pl.when(core_ref[0] == 0)
    def _():
        sums((keep_ref, send_ref))

    @pl.when(core_ref[0] == 1)
    def _():
        sums((send_ref, keep_ref))


def project_far(core, near, left, waves, pieces):
    half = jax.ShapeDtypeStruct((NP, NB_DEV), F32)
    return pl.pallas_call(
        far_kernel,
        out_shape=(half, half),
        in_specs=[smem()] + [vmem()] * 7,
        out_specs=(vmem(), vmem()),
        scratch_shapes=[pltpu.VMEM((NP, NPW_DEV), BF16)],
        compiler_params=params(16),
        cost_estimate=cost(4 * NP * NPW_DEV * NB_DEV, 6 * MIB),
    )(core, near, left, waves, *pieces)


def turn_kernel(*refs):
    pieces, (out_ref, rows_ref) = refs[:8], refs[8:]
    for i, piece in enumerate(pieces):
        at = (i // 4) * HALF + (3 - i % 4) * ROWS
        for k in range(2):
            rows_ref[pl.ds(k * NP + at, ROWS), :] = piece[k]
    turned = rows_ref[...].T
    first, second = turned[:, :NP], turned[:, NP:]
    out_ref[0, :, :NP] = first
    out_ref[0, :, NP:] = -second
    out_ref[1, :, :NP] = second
    out_ref[1, :, NP:] = first


def turn(pieces):
    return pl.pallas_call(
        turn_kernel,
        out_shape=jax.ShapeDtypeStruct((2, NPW_DEV, 2 * NP), BF16),
        in_specs=[vmem()] * 8,
        out_specs=vmem(),
        scratch_shapes=[pltpu.VMEM((2 * NP, NPW_DEV), BF16)],
        compiler_params=params(16),
        cost_estimate=cost(2 * NP * NPW_DEV, 2 * MIB),
    )(*pieces)


def spread_kernel(
    core_ref, y_ref, own_ref, other_ref, turned_ref, out_ref, right_ref, result_ref, sem
):
    core, y = core_ref[0], y_ref[0]
    for s in range(4):
        at = jnp.bitwise_xor(y, s) * CHUNK
        own_at = pl.multiple_of(core * NP + at, CHUNK)
        other_at = pl.multiple_of((1 - core) * NP + at, CHUNK)
        right_ref[pl.ds(own_at, CHUNK), :] = own_ref[s]
        right_ref[pl.ds(other_at, CHUNK), :] = other_ref[s]
    right = right_ref[...]
    copies = []
    for k in range(2):
        for at in range(0, NPW_DEV, BLOCK_PW):
            rows = pl.ds(at, BLOCK_PW)
            result_ref[k, rows, :] = jnp.dot(
                turned_ref[k, rows, :], right, preferred_element_type=F32
            ).astype(BF16)
            copy = pltpu.make_async_copy(
                result_ref.at[k, rows], out_ref.at[k, rows], sem.at[len(copies)]
            )
            copy.start()
            copies.append(copy)
    for copy in copies:
        copy.wait()


def spread_back(core, y, own, other, turned):
    return pl.pallas_call(
        spread_kernel,
        out_shape=jax.ShapeDtypeStruct((2, NPW_DEV, NB_DEV), BF16),
        in_specs=[smem(), smem()] + [vmem()] * 3,
        out_specs=pl.BlockSpec(memory_space=pltpu.HBM),
        scratch_shapes=[
            pltpu.VMEM((2 * NP, NB_DEV), BF16),
            pltpu.VMEM((2, NPW_DEV, NB_DEV), BF16),
            pltpu.SemaphoreType.DMA((2 * NPW_DEV // BLOCK_PW,)),
        ],
        compiler_params=params(16),
        cost_estimate=cost(8 * NP * NPW_DEV * NB_DEV, 6 * MIB),
    )(core, y, own, other, turned)


def shards(waves, projectors, coupling, offsets, counts):
    pw, band = lax.axis_index("pw"), lax.axis_index("band")
    core, y, band = (i.reshape(1) for i in (pw & 1, (pw >> 1) & 3, band))

    distant = over_band(projectors, 1)
    near = [over_band(projectors, bits) for bits in (6, 4, 2)] + [projectors]
    far = [over_band(distant, bits) for bits in (6, 4, 2)] + [distant]
    pick = gathered_order(y, band)
    pick, _ = lax.optimization_barrier((pick, distant))
    left, waves = ahead(pick, offsets, counts, coupling, waves)
    sums = project_near(left, waves, near)
    keep, send = project_far(core, sums, left, waves, far)
    turned = turn(near + far)
    total = (keep + over_pw(send, 1)).reshape(4, CHUNK, NB_DEV)

    sums = total[0]
    for arrived in [over_pw(total[s].astype(BF16), 2 * s) for s in (3, 2, 1)]:
        sums = sums + arrived.astype(F32)
    sent = sums.astype(BF16)
    for arrived in [over_pw(sent, 8 * s) for s in (3, 2, 1)]:
        sums = sums + arrived.astype(F32)
    mine = sums.astype(BF16)
    chunk = {s: over_pw(mine, 2 * s) for s in (3, 2, 1)}
    own = jnp.stack([mine, chunk[1], chunk[2], chunk[3]])
    other = over_pw(own, 1)
    return spread_back(core, y, own, other, turned)


def solution(mesh):
    placed = (P(None, "pw", "band"), P(None, "band", "pw"), P(), P(), P())
    return jax.shard_map(
        shards, mesh=mesh, in_specs=placed, out_specs=P(None, "pw", "band"), check_vma=False
    )
```

```python
import jax
import jax.numpy as jnp
from jax import lax
from jax.experimental import pallas as pl
from jax.experimental.pallas import tpu as pltpu
from jax.sharding import PartitionSpec as P

NP = 128
NATOM = 12
M = 13
ROWS = 16
HALF = 64
NPW_DEV = 1280
NB_DEV = 896
CHUNK = 32
SLOTS = (0, 2, 3, 1)
BLOCK_PW = 640
BF16 = jnp.bfloat16
F32 = jnp.float32
MIB = 1024 * 1024


def over_pw(x, bits):
    return lax.ppermute(x, "pw", [(i, i ^ bits) for i in range(32)])


def over_band(x, bits):
    return lax.ppermute(x, "band", [(i, i ^ bits) for i in range(8)])


def vmem():
    return pl.BlockSpec(memory_space=pltpu.VMEM)


def smem():
    return pl.BlockSpec(memory_space=pltpu.SMEM)


def params(mib):
    return pltpu.CompilerParams(vmem_limit_bytes=mib * MIB)


def cost(flops, nbytes):
    return pl.CostEstimate(flops=flops, bytes_accessed=nbytes, transcendentals=0)


def two_terms(x):
    high = x.astype(BF16)
    return high, (x - high.astype(F32)).astype(BF16)


def ahead_kernel(
    pick_ref,
    offsets_hbm,
    counts_hbm,
    coupling_hbm,
    waves_hbm,
    left_ref,
    waves_ref,
    placed_ref,
    offsets_ref,
    counts_ref,
    coupling_ref,
    sem,
):
    pairs = (
        (offsets_hbm, offsets_ref),
        (counts_hbm, counts_ref),
        (coupling_hbm, coupling_ref),
        (waves_hbm, waves_ref),
    )
    copies = [pltpu.make_async_copy(a, b, sem.at[i]) for i, (a, b) in enumerate(pairs)]
    for copy in copies:
        copy.start()
    placed_ref[...] = jnp.zeros(placed_ref.shape, F32)
    for copy in copies[:3]:
        copy.wait()
    row = lax.broadcasted_iota(jnp.int32, (M, NP), 0)
    column = lax.broadcasted_iota(jnp.int32, (M, NP), 1)
    for atom in range(NATOM):
        at, count = offsets_ref[atom], counts_ref[atom]
        wide = jnp.concatenate([coupling_ref[atom], jnp.zeros((M, NP - M), F32)], axis=1)
        wide = jnp.where((row < count) & (column < count), wide, 0.0)
        placed_ref[pl.ds(at, M), :] = pltpu.roll(wide, at, 1)
    placed = placed_ref[:NP, :]
    block = (placed + placed.T) * 0.5
    pick, pick_turned = pick_ref[0], pick_ref[1]

    def reorder(part):
        part = jnp.dot(part, pick, preferred_element_type=F32).astype(BF16)
        return jnp.dot(pick_turned, part, preferred_element_type=F32).astype(BF16)

    high, low = (reorder(part) for part in two_terms(block))
    for h in range(2):
        columns = slice(h * HALF, (h + 1) * HALF)
        left_ref[h] = jnp.concatenate(
            [high[:, columns], high[:, columns], low[:, columns]], axis=1
        )
    copies[3].wait()


def pick_kernel(y_ref, band_ref, pick_ref):
    def pick(place):
        piece = place >> 4
        piece = ((piece & 3) << 1) | (piece >> 2)
        number = (jnp.bitwise_xor(piece, band_ref[0]) << 4) | (place & 15)
        projector = lax.broadcasted_iota(jnp.int32, (NP, NP), 0)
        return (projector == number).astype(F32)

    place = lax.broadcasted_iota(jnp.int32, (NP, NP), 1)
    pick_ref[0] = pick(place).astype(BF16)
    pick_ref[1] = pick(jnp.bitwise_xor(place, y_ref[0] << 5)).T.astype(BF16)


def gathered_order(y, band):
    return pl.pallas_call(
        pick_kernel,
        out_shape=jax.ShapeDtypeStruct((2, NP, NP), BF16),
        in_specs=[smem(), smem()],
        out_specs=vmem(),
        compiler_params=params(8),
        cost_estimate=cost(4 * 10**9, 1),
    )(y, band)


def ahead(pick, offsets, counts, coupling, waves):
    hbm = pl.BlockSpec(memory_space=pltpu.HBM)
    return pl.pallas_call(
        ahead_kernel,
        out_shape=(
            jax.ShapeDtypeStruct((2, NP, 3 * HALF), BF16),
            jax.ShapeDtypeStruct(waves.shape, BF16),
        ),
        in_specs=[vmem()] + [hbm] * 4,
        out_specs=(vmem(), vmem()),
        scratch_shapes=[
            pltpu.VMEM((NP + ROWS, NP), F32),
            pltpu.SMEM((NATOM,), jnp.int32),
            pltpu.SMEM((NATOM,), jnp.int32),
            pltpu.VMEM((NATOM, M, M), F32),
            pltpu.SemaphoreType.DMA((4,)),
        ],
        compiler_params=params(46),
        cost_estimate=cost(2 * 10**9, 8 * MIB),
    )(pick, offsets, counts, coupling, waves)


def coupled_parts(h, pieces, left_ref, waves_ref, rows_ref):
    for i, piece in enumerate(pieces):
        at = (3 - i) * ROWS
        rows_ref[pl.ds(at, ROWS), :] = piece[0]
        rows_ref[pl.ds(HALF + at, ROWS), :] = piece[1]
    rows = rows_ref[...]
    first = jnp.dot(rows, waves_ref[0], preferred_element_type=F32)
    second = jnp.dot(rows, waves_ref[1], preferred_element_type=F32)
    left = left_ref[h]

    def couple(part):
        high, low = two_terms(part)
        right = jnp.concatenate([high, low, high], axis=0)
        return jnp.dot(left, right, preferred_element_type=F32)

    return couple(first[:HALF] + second[HALF:]), couple(second[:HALF] - first[HALF:])


def near_kernel(left_ref, waves_ref, *refs):
    pieces, (out_ref, rows_ref) = refs[:4], refs[4:]
    out_ref[0], out_ref[1] = coupled_parts(0, pieces, left_ref, waves_ref, rows_ref)


def project_near(left, waves, pieces):
    return pl.pallas_call(
        near_kernel,
        out_shape=jax.ShapeDtypeStruct((2, NP, NB_DEV), F32),
        in_specs=[vmem()] * 6,
        out_specs=vmem(),
        scratch_shapes=[pltpu.VMEM((NP, NPW_DEV), BF16)],
        compiler_params=params(16),
        cost_estimate=cost(4 * NP * NPW_DEV * NB_DEV, 6 * MIB),
    )(left, waves, *pieces)


def far_kernel(core_ref, near_ref, left_ref, waves_ref, *refs):
    pieces, (keep_ref, send_ref, rows_ref) = refs[:4], refs[4:]

    def sums(out_refs):
        parts = coupled_parts(1, pieces, left_ref, waves_ref, rows_ref)
        for k in range(2):
            out_refs[k][...] = parts[k] + near_ref[k]

    @pl.when(core_ref[0] == 0)
    def _():
        sums((keep_ref, send_ref))

    @pl.when(core_ref[0] == 1)
    def _():
        sums((send_ref, keep_ref))


def project_far(core, near, left, waves, pieces):
    half = jax.ShapeDtypeStruct((NP, NB_DEV), F32)
    return pl.pallas_call(
        far_kernel,
        out_shape=(half, half),
        in_specs=[smem()] + [vmem()] * 7,
        out_specs=(vmem(), vmem()),
        scratch_shapes=[pltpu.VMEM((NP, NPW_DEV), BF16)],
        compiler_params=params(16),
        cost_estimate=cost(4 * NP * NPW_DEV * NB_DEV, 6 * MIB),
    )(core, near, left, waves, *pieces)


def turn_kernel(*refs):
    pieces, (out_ref, rows_ref) = refs[:8], refs[8:]
    for i, piece in enumerate(pieces):
        at = (i // 4) * HALF + (3 - i % 4) * ROWS
        for k in range(2):
            rows_ref[pl.ds(k * NP + at, ROWS), :] = piece[k]
    turned = rows_ref[...].T
    first, second = turned[:, :NP], turned[:, NP:]
    out_ref[0, :, :NP] = first
    out_ref[0, :, NP:] = -second
    out_ref[1, :, :NP] = second
    out_ref[1, :, NP:] = first


def turn(pieces):
    return pl.pallas_call(
        turn_kernel,
        out_shape=jax.ShapeDtypeStruct((2, NPW_DEV, 2 * NP), BF16),
        in_specs=[vmem()] * 8,
        out_specs=vmem(),
        scratch_shapes=[pltpu.VMEM((2 * NP, NPW_DEV), BF16)],
        compiler_params=params(16),
        cost_estimate=cost(2 * NP * NPW_DEV, 2 * MIB),
    )(*pieces)


def spread_kernel(
    core_ref, y_ref, own_ref, other_ref, turned_ref, out_ref, right_ref, result_ref, sem
):
    core, y = core_ref[0], y_ref[0]
    for s, slot in enumerate(SLOTS):
        at = jnp.bitwise_xor(y, slot) * CHUNK
        own_at = pl.multiple_of(core * NP + at, CHUNK)
        other_at = pl.multiple_of((1 - core) * NP + at, CHUNK)
        right_ref[pl.ds(own_at, CHUNK), :] = own_ref[s]
        right_ref[pl.ds(other_at, CHUNK), :] = other_ref[s]
    right = right_ref[...]
    copies = []
    for k in range(2):
        for at in range(0, NPW_DEV, BLOCK_PW):
            rows = pl.ds(at, BLOCK_PW)
            result_ref[k, rows, :] = jnp.dot(
                turned_ref[k, rows, :], right, preferred_element_type=F32
            ).astype(BF16)
            copy = pltpu.make_async_copy(
                result_ref.at[k, rows], out_ref.at[k, rows], sem.at[len(copies)]
            )
            copy.start()
            copies.append(copy)
    for copy in copies:
        copy.wait()


def spread_back(core, y, own, other, turned):
    return pl.pallas_call(
        spread_kernel,
        out_shape=jax.ShapeDtypeStruct((2, NPW_DEV, NB_DEV), BF16),
        in_specs=[smem(), smem()] + [vmem()] * 3,
        out_specs=pl.BlockSpec(memory_space=pltpu.HBM),
        scratch_shapes=[
            pltpu.VMEM((2 * NP, NB_DEV), BF16),
            pltpu.VMEM((2, NPW_DEV, NB_DEV), BF16),
            pltpu.SemaphoreType.DMA((2 * NPW_DEV // BLOCK_PW,)),
        ],
        compiler_params=params(16),
        cost_estimate=cost(8 * NP * NPW_DEV * NB_DEV, 6 * MIB),
    )(core, y, own, other, turned)


def shards(waves, projectors, coupling, offsets, counts):
    pw, band = lax.axis_index("pw"), lax.axis_index("band")
    core, y, band = (i.reshape(1) for i in (pw & 1, (pw >> 1) & 3, band))

    distant = over_band(projectors, 1)
    near = [over_band(projectors, bits) for bits in (6, 4, 2)] + [projectors]
    far = [over_band(distant, bits) for bits in (6, 4, 2)] + [distant]
    pick = gathered_order(y, band)
    pick, _ = lax.optimization_barrier((pick, distant))
    left, waves = ahead(pick, offsets, counts, coupling, waves)
    sums = project_near(left, waves, near)
    keep, send = project_far(core, sums, left, waves, far)
    turned = turn(near + far)
    total = (keep + over_pw(send, 1)).reshape(4, CHUNK, NB_DEV)

    sums = total[0]
    for arrived in [over_pw(total[s].astype(BF16), 2 * s) for s in (3, 1, 2)]:
        sums = sums + arrived.astype(F32)
    sent = sums.astype(BF16)
    for arrived in [over_pw(sent, 8 * s) for s in (3, 2, 1)]:
        sums = sums + arrived.astype(F32)
    mine = sums.astype(BF16)
    own = jnp.stack([mine] + [over_pw(mine, 2 * s) for s in SLOTS[1:]])
    other = over_pw(own, 1)
    return spread_back(core, y, own, other, turned)


def solution(mesh):
    placed = (P(None, "pw", "band"), P(None, "band", "pw"), P(), P(), P())
    return jax.shard_map(
        shards, mesh=mesh, in_specs=placed, out_specs=P(None, "pw", "band"), check_vma=False
    )
```

```python
import jax
import jax.numpy as jnp
from jax import lax
from jax.experimental import pallas as pl
from jax.experimental.pallas import tpu as pltpu
from jax.sharding import PartitionSpec as P

NP = 128
NATOM = 12
M = 13
ROWS = 16
HALF = 64
NPW_DEV = 1280
NB_DEV = 896
CHUNK = 32
SLOTS = (0, 2, 3, 1)
BLOCK_PW = 320
BF16 = jnp.bfloat16
F32 = jnp.float32
MIB = 1024 * 1024


def over_pw(x, bits):
    return lax.ppermute(x, "pw", [(i, i ^ bits) for i in range(32)])


def over_band(x, bits):
    return lax.ppermute(x, "band", [(i, i ^ bits) for i in range(8)])


def vmem():
    return pl.BlockSpec(memory_space=pltpu.VMEM)


def smem():
    return pl.BlockSpec(memory_space=pltpu.SMEM)


def params(mib):
    return pltpu.CompilerParams(vmem_limit_bytes=mib * MIB)


def cost(flops, nbytes):
    return pl.CostEstimate(flops=flops, bytes_accessed=nbytes, transcendentals=0)


def two_terms(x):
    high = x.astype(BF16)
    return high, (x - high.astype(F32)).astype(BF16)


def ahead_kernel(
    pick_ref,
    offsets_hbm,
    counts_hbm,
    coupling_hbm,
    waves_hbm,
    left_ref,
    waves_ref,
    placed_ref,
    offsets_ref,
    counts_ref,
    coupling_ref,
    sem,
):
    pairs = (
        (offsets_hbm, offsets_ref),
        (counts_hbm, counts_ref),
        (coupling_hbm, coupling_ref),
        (waves_hbm, waves_ref),
    )
    copies = [pltpu.make_async_copy(a, b, sem.at[i]) for i, (a, b) in enumerate(pairs)]
    for copy in copies:
        copy.start()
    placed_ref[...] = jnp.zeros(placed_ref.shape, F32)
    for copy in copies[:3]:
        copy.wait()
    row = lax.broadcasted_iota(jnp.int32, (M, NP), 0)
    column = lax.broadcasted_iota(jnp.int32, (M, NP), 1)
    for atom in range(NATOM):
        at, count = offsets_ref[atom], counts_ref[atom]
        wide = jnp.concatenate([coupling_ref[atom], jnp.zeros((M, NP - M), F32)], axis=1)
        wide = jnp.where((row < count) & (column < count), wide, 0.0)
        placed_ref[pl.ds(at, M), :] = pltpu.roll(wide, at, 1)
    placed = placed_ref[:NP, :]
    block = (placed + placed.T) * 0.5
    pick, pick_turned = pick_ref[0], pick_ref[1]

    def reorder(part):
        part = jnp.dot(part, pick, preferred_element_type=F32).astype(BF16)
        return jnp.dot(pick_turned, part, preferred_element_type=F32).astype(BF16)

    high, low = (reorder(part) for part in two_terms(block))
    for h in range(2):
        columns = slice(h * HALF, (h + 1) * HALF)
        left_ref[h] = jnp.concatenate(
            [high[:, columns], high[:, columns], low[:, columns]], axis=1
        )
    copies[3].wait()


def pick_kernel(y_ref, band_ref, pick_ref):
    def pick(place):
        piece = place >> 4
        piece = ((piece & 3) << 1) | (piece >> 2)
        number = (jnp.bitwise_xor(piece, band_ref[0]) << 4) | (place & 15)
        projector = lax.broadcasted_iota(jnp.int32, (NP, NP), 0)
        return (projector == number).astype(F32)

    place = lax.broadcasted_iota(jnp.int32, (NP, NP), 1)
    pick_ref[0] = pick(place).astype(BF16)
    pick_ref[1] = pick(jnp.bitwise_xor(place, y_ref[0] << 5)).T.astype(BF16)


def gathered_order(y, band):
    return pl.pallas_call(
        pick_kernel,
        out_shape=jax.ShapeDtypeStruct((2, NP, NP), BF16),
        in_specs=[smem(), smem()],
        out_specs=vmem(),
        compiler_params=params(8),
        cost_estimate=cost(4 * 10**9, 1),
    )(y, band)


def ahead(pick, offsets, counts, coupling, waves):
    hbm = pl.BlockSpec(memory_space=pltpu.HBM)
    return pl.pallas_call(
        ahead_kernel,
        out_shape=(
            jax.ShapeDtypeStruct((2, NP, 3 * HALF), BF16),
            jax.ShapeDtypeStruct(waves.shape, BF16),
        ),
        in_specs=[vmem()] + [hbm] * 4,
        out_specs=(vmem(), vmem()),
        scratch_shapes=[
            pltpu.VMEM((NP + ROWS, NP), F32),
            pltpu.SMEM((NATOM,), jnp.int32),
            pltpu.SMEM((NATOM,), jnp.int32),
            pltpu.VMEM((NATOM, M, M), F32),
            pltpu.SemaphoreType.DMA((4,)),
        ],
        compiler_params=params(46),
        cost_estimate=cost(2 * 10**9, 8 * MIB),
    )(pick, offsets, counts, coupling, waves)


def coupled_parts(h, pieces, left_ref, waves_ref, rows_ref):
    for i, piece in enumerate(pieces):
        at = (3 - i) * ROWS
        rows_ref[pl.ds(at, ROWS), :] = piece[0]
        rows_ref[pl.ds(HALF + at, ROWS), :] = piece[1]
    rows = rows_ref[...]
    first = jnp.dot(rows, waves_ref[0], preferred_element_type=F32)
    second = jnp.dot(rows, waves_ref[1], preferred_element_type=F32)
    left = left_ref[h]

    def couple(part):
        high, low = two_terms(part)
        right = jnp.concatenate([high, low, high], axis=0)
        return jnp.dot(left, right, preferred_element_type=F32)

    return couple(first[:HALF] + second[HALF:]), couple(second[:HALF] - first[HALF:])


def near_kernel(left_ref, waves_ref, *refs):
    pieces, (out_ref, rows_ref) = refs[:4], refs[4:]
    out_ref[0], out_ref[1] = coupled_parts(0, pieces, left_ref, waves_ref, rows_ref)


def project_near(left, waves, pieces):
    return pl.pallas_call(
        near_kernel,
        out_shape=jax.ShapeDtypeStruct((2, NP, NB_DEV), F32),
        in_specs=[vmem()] * 6,
        out_specs=vmem(),
        scratch_shapes=[pltpu.VMEM((NP, NPW_DEV), BF16)],
        compiler_params=params(16),
        cost_estimate=cost(4 * NP * NPW_DEV * NB_DEV, 6 * MIB),
    )(left, waves, *pieces)


def far_kernel(core_ref, near_ref, left_ref, waves_ref, *refs):
    pieces, (keep_ref, send_ref, rows_ref) = refs[:4], refs[4:]

    def sums(out_refs):
        parts = coupled_parts(1, pieces, left_ref, waves_ref, rows_ref)
        for k in range(2):
            out_refs[k][...] = parts[k] + near_ref[k]

    @pl.when(core_ref[0] == 0)
    def _():
        sums((keep_ref, send_ref))

    @pl.when(core_ref[0] == 1)
    def _():
        sums((send_ref, keep_ref))


def project_far(core, near, left, waves, pieces):
    half = jax.ShapeDtypeStruct((NP, NB_DEV), F32)
    return pl.pallas_call(
        far_kernel,
        out_shape=(half, half),
        in_specs=[smem()] + [vmem()] * 7,
        out_specs=(vmem(), vmem()),
        scratch_shapes=[pltpu.VMEM((NP, NPW_DEV), BF16)],
        compiler_params=params(16),
        cost_estimate=cost(4 * NP * NPW_DEV * NB_DEV, 6 * MIB),
    )(core, near, left, waves, *pieces)


def turn_kernel(*refs):
    pieces, (out_ref, rows_ref) = refs[:8], refs[8:]
    for i, piece in enumerate(pieces):
        at = (i // 4) * HALF + (3 - i % 4) * ROWS
        for k in range(2):
            rows_ref[pl.ds(k * NP + at, ROWS), :] = piece[k]
    turned = rows_ref[...].T
    first, second = turned[:, :NP], turned[:, NP:]
    out_ref[0, :, :NP] = first
    out_ref[0, :, NP:] = -second
    out_ref[1, :, :NP] = second
    out_ref[1, :, NP:] = first


def turn(pieces):
    return pl.pallas_call(
        turn_kernel,
        out_shape=jax.ShapeDtypeStruct((2, NPW_DEV, 2 * NP), BF16),
        in_specs=[vmem()] * 8,
        out_specs=vmem(),
        scratch_shapes=[pltpu.VMEM((2 * NP, NPW_DEV), BF16)],
        compiler_params=params(16),
        cost_estimate=cost(2 * NP * NPW_DEV, 2 * MIB),
    )(*pieces)


def spread_kernel(
    core_ref, y_ref, own_ref, other_ref, turned_ref, out_ref, right_ref, result_ref, sem
):
    core, y = core_ref[0], y_ref[0]
    for s, slot in enumerate(SLOTS):
        at = jnp.bitwise_xor(y, slot) * CHUNK
        own_at = pl.multiple_of(core * NP + at, CHUNK)
        other_at = pl.multiple_of((1 - core) * NP + at, CHUNK)
        right_ref[pl.ds(own_at, CHUNK), :] = own_ref[s]
        right_ref[pl.ds(other_at, CHUNK), :] = other_ref[s]
    right = right_ref[...]
    copies = []
    for k in range(2):
        for at in range(0, NPW_DEV, BLOCK_PW):
            rows = pl.ds(at, BLOCK_PW)
            result_ref[k, rows, :] = jnp.dot(
                turned_ref[k, rows, :], right, preferred_element_type=F32
            ).astype(BF16)
            copy = pltpu.make_async_copy(
                result_ref.at[k, rows], out_ref.at[k, rows], sem.at[len(copies)]
            )
            copy.start()
            copies.append(copy)
    for copy in copies:
        copy.wait()


def spread_back(core, y, own, other, turned):
    return pl.pallas_call(
        spread_kernel,
        out_shape=jax.ShapeDtypeStruct((2, NPW_DEV, NB_DEV), BF16),
        in_specs=[smem(), smem()] + [vmem()] * 3,
        out_specs=pl.BlockSpec(memory_space=pltpu.HBM),
        scratch_shapes=[
            pltpu.VMEM((2 * NP, NB_DEV), BF16),
            pltpu.VMEM((2, NPW_DEV, NB_DEV), BF16),
            pltpu.SemaphoreType.DMA((2 * NPW_DEV // BLOCK_PW,)),
        ],
        compiler_params=params(16),
        cost_estimate=cost(8 * NP * NPW_DEV * NB_DEV, 6 * MIB),
    )(core, y, own, other, turned)


def shards(waves, projectors, coupling, offsets, counts):
    pw, band = lax.axis_index("pw"), lax.axis_index("band")
    core, y, band = (i.reshape(1) for i in (pw & 1, (pw >> 1) & 3, band))

    distant = over_band(projectors, 1)
    near = [over_band(projectors, bits) for bits in (6, 4, 2)] + [projectors]
    far = [over_band(distant, bits) for bits in (6, 4, 2)] + [distant]
    pick = gathered_order(y, band)
    pick, _ = lax.optimization_barrier((pick, distant))
    left, waves = ahead(pick, offsets, counts, coupling, waves)
    sums = project_near(left, waves, near)
    keep, send = project_far(core, sums, left, waves, far)
    turned = turn(near + far)
    total = (keep + over_pw(send, 1)).reshape(4, CHUNK, NB_DEV)

    sums = total[0]
    for arrived in [over_pw(total[s].astype(BF16), 2 * s) for s in (3, 1, 2)]:
        sums = sums + arrived.astype(F32)
    sent = sums.astype(BF16)
    for arrived in [over_pw(sent, 8 * s) for s in (3, 1, 2)]:
        sums = sums + arrived.astype(F32)
    mine = sums.astype(BF16)
    own = jnp.stack([mine] + [over_pw(mine, 2 * s) for s in SLOTS[1:]])
    other = over_pw(own, 1)
    return spread_back(core, y, own, other, turned)


def solution(mesh):
    placed = (P(None, "pw", "band"), P(None, "band", "pw"), P(), P(), P())
    return jax.shard_map(
        shards, mesh=mesh, in_specs=placed, out_specs=P(None, "pw", "band"), check_vma=False
    )
```

```python
import jax
import jax.numpy as jnp
from jax import lax
from jax.experimental import pallas as pl
from jax.experimental.pallas import tpu as pltpu
from jax.sharding import PartitionSpec as P

NP = 128
NATOM = 12
M = 13
ROWS = 16
HALF = 64
NPW_DEV = 1280
NB_DEV = 896
CHUNK = 32
SLOTS = (0, 2, 3, 1)
BLOCK_PW = 320
BF16 = jnp.bfloat16
F32 = jnp.float32
MIB = 1024 * 1024


def over_pw(x, bits):
    return lax.ppermute(x, "pw", [(i, i ^ bits) for i in range(32)])


def over_band(x, bits):
    return lax.ppermute(x, "band", [(i, i ^ bits) for i in range(8)])


def vmem():
    return pl.BlockSpec(memory_space=pltpu.VMEM)


def smem():
    return pl.BlockSpec(memory_space=pltpu.SMEM)


def params(mib):
    return pltpu.CompilerParams(vmem_limit_bytes=mib * MIB)


def cost(flops, nbytes):
    return pl.CostEstimate(flops=flops, bytes_accessed=nbytes, transcendentals=0)


def two_terms(x):
    high = x.astype(BF16)
    return high, (x - high.astype(F32)).astype(BF16)


def ahead_kernel(
    pick_ref,
    offsets_hbm,
    counts_hbm,
    coupling_hbm,
    waves_hbm,
    left_ref,
    waves_ref,
    placed_ref,
    offsets_ref,
    counts_ref,
    coupling_ref,
    sem,
):
    pairs = (
        (offsets_hbm, offsets_ref),
        (counts_hbm, counts_ref),
        (coupling_hbm, coupling_ref),
        (waves_hbm, waves_ref),
    )
    copies = [pltpu.make_async_copy(a, b, sem.at[i]) for i, (a, b) in enumerate(pairs)]
    for copy in copies:
        copy.start()
    placed_ref[...] = jnp.zeros(placed_ref.shape, F32)
    for copy in copies[:3]:
        copy.wait()
    row = lax.broadcasted_iota(jnp.int32, (M, NP), 0)
    column = lax.broadcasted_iota(jnp.int32, (M, NP), 1)
    for atom in range(NATOM):
        at, count = offsets_ref[atom], counts_ref[atom]
        wide = jnp.concatenate([coupling_ref[atom], jnp.zeros((M, NP - M), F32)], axis=1)
        wide = jnp.where((row < count) & (column < count), wide, 0.0)
        placed_ref[pl.ds(at, M), :] = pltpu.roll(wide, at, 1)
    placed = placed_ref[:NP, :]
    block = (placed + placed.T) * 0.5
    pick, pick_turned = pick_ref[0], pick_ref[1]

    def reorder(part):
        part = jnp.dot(part, pick, preferred_element_type=F32).astype(BF16)
        return jnp.dot(pick_turned, part, preferred_element_type=F32).astype(BF16)

    high, low = (reorder(part) for part in two_terms(block))
    for h in range(2):
        columns = slice(h * HALF, (h + 1) * HALF)
        left_ref[h] = jnp.concatenate(
            [high[:, columns], high[:, columns], low[:, columns]], axis=1
        )
    copies[3].wait()


def pick_kernel(y_ref, band_ref, pick_ref):
    def pick(place):
        piece = place >> 4
        piece = ((piece & 3) << 1) | (piece >> 2)
        number = (jnp.bitwise_xor(piece, band_ref[0]) << 4) | (place & 15)
        projector = lax.broadcasted_iota(jnp.int32, (NP, NP), 0)
        return (projector == number).astype(F32)

    place = lax.broadcasted_iota(jnp.int32, (NP, NP), 1)
    pick_ref[0] = pick(place).astype(BF16)
    pick_ref[1] = pick(jnp.bitwise_xor(place, y_ref[0] << 5)).T.astype(BF16)


def gathered_order(y, band):
    return pl.pallas_call(
        pick_kernel,
        out_shape=jax.ShapeDtypeStruct((2, NP, NP), BF16),
        in_specs=[smem(), smem()],
        out_specs=vmem(),
        compiler_params=params(8),
        cost_estimate=cost(4 * 10**9, 1),
    )(y, band)


def ahead(pick, offsets, counts, coupling, waves):
    hbm = pl.BlockSpec(memory_space=pltpu.HBM)
    return pl.pallas_call(
        ahead_kernel,
        out_shape=(
            jax.ShapeDtypeStruct((2, NP, 3 * HALF), BF16),
            jax.ShapeDtypeStruct(waves.shape, BF16),
        ),
        in_specs=[vmem()] + [hbm] * 4,
        out_specs=(vmem(), vmem()),
        scratch_shapes=[
            pltpu.VMEM((NP + ROWS, NP), F32),
            pltpu.SMEM((NATOM,), jnp.int32),
            pltpu.SMEM((NATOM,), jnp.int32),
            pltpu.VMEM((NATOM, M, M), F32),
            pltpu.SemaphoreType.DMA((4,)),
        ],
        compiler_params=params(46),
        cost_estimate=cost(2 * 10**9, 8 * MIB),
    )(pick, offsets, counts, coupling, waves)


def coupled_parts(h, pieces, left_ref, waves_ref, rows_ref):
    for i, piece in enumerate(pieces):
        at = (3 - i) * ROWS
        rows_ref[pl.ds(at, ROWS), :] = piece[0]
        rows_ref[pl.ds(HALF + at, ROWS), :] = piece[1]
    rows = rows_ref[...]
    first = jnp.dot(rows, waves_ref[0], preferred_element_type=F32)
    second = jnp.dot(rows, waves_ref[1], preferred_element_type=F32)
    left = left_ref[h]

    def couple(part):
        high, low = two_terms(part)
        right = jnp.concatenate([high, low, high], axis=0)
        return jnp.dot(left, right, preferred_element_type=F32)

    return couple(first[:HALF] + second[HALF:]), couple(second[:HALF] - first[HALF:])


def near_kernel(left_ref, waves_ref, *refs):
    pieces, (out_ref, rows_ref) = refs[:4], refs[4:]
    out_ref[0], out_ref[1] = coupled_parts(0, pieces, left_ref, waves_ref, rows_ref)


def project_near(left, waves, pieces):
    return pl.pallas_call(
        near_kernel,
        out_shape=jax.ShapeDtypeStruct((2, NP, NB_DEV), F32),
        in_specs=[vmem()] * 6,
        out_specs=vmem(),
        scratch_shapes=[pltpu.VMEM((NP, NPW_DEV), BF16)],
        compiler_params=params(16),
        cost_estimate=cost(4 * NP * NPW_DEV * NB_DEV, 6 * MIB),
    )(left, waves, *pieces)


def far_kernel(core_ref, near_ref, left_ref, waves_ref, *refs):
    pieces, (keep_ref, send_ref, rows_ref) = refs[:4], refs[4:]

    def sums(out_refs):
        parts = coupled_parts(1, pieces, left_ref, waves_ref, rows_ref)
        for k in range(2):
            out_refs[k][...] = (parts[k] + near_ref[k]).astype(out_refs[k].dtype)

    @pl.when(core_ref[0] == 0)
    def _():
        sums((keep_ref, send_ref))

    @pl.when(core_ref[0] == 1)
    def _():
        sums((send_ref, keep_ref))


def project_far(core, near, left, waves, pieces):
    halves = [jax.ShapeDtypeStruct((NP, NB_DEV), dtype) for dtype in (F32, BF16)]
    return pl.pallas_call(
        far_kernel,
        out_shape=halves,
        in_specs=[smem()] + [vmem()] * 7,
        out_specs=(vmem(), vmem()),
        scratch_shapes=[pltpu.VMEM((NP, NPW_DEV), BF16)],
        compiler_params=params(16),
        cost_estimate=cost(4 * NP * NPW_DEV * NB_DEV, 6 * MIB),
    )(core, near, left, waves, *pieces)


def turn_kernel(*refs):
    pieces, (out_ref, rows_ref) = refs[:8], refs[8:]
    for i, piece in enumerate(pieces):
        at = (i // 4) * HALF + (3 - i % 4) * ROWS
        for k in range(2):
            rows_ref[pl.ds(k * NP + at, ROWS), :] = piece[k]
    turned = rows_ref[...].T
    first, second = turned[:, :NP], turned[:, NP:]
    out_ref[0, :, :NP] = first
    out_ref[0, :, NP:] = -second
    out_ref[1, :, :NP] = second
    out_ref[1, :, NP:] = first


def turn(pieces):
    return pl.pallas_call(
        turn_kernel,
        out_shape=jax.ShapeDtypeStruct((2, NPW_DEV, 2 * NP), BF16),
        in_specs=[vmem()] * 8,
        out_specs=vmem(),
        scratch_shapes=[pltpu.VMEM((2 * NP, NPW_DEV), BF16)],
        compiler_params=params(16),
        cost_estimate=cost(2 * NP * NPW_DEV, 2 * MIB),
    )(*pieces)


def spread_kernel(core_ref, y_ref, *refs):
    own_ref, other_ref = refs[:4], refs[4:8]
    turned_ref, out_ref, right_ref, result_ref, sem = refs[8:]
    core, y = core_ref[0], y_ref[0]
    for s, slot in enumerate(SLOTS):
        at = jnp.bitwise_xor(y, slot) * CHUNK
        own_at = pl.multiple_of(core * NP + at, CHUNK)
        other_at = pl.multiple_of((1 - core) * NP + at, CHUNK)
        right_ref[pl.ds(own_at, CHUNK), :] = own_ref[s][...]
        right_ref[pl.ds(other_at, CHUNK), :] = other_ref[s][...]
    right = right_ref[...]
    copies = []
    for k in range(2):
        for at in range(0, NPW_DEV, BLOCK_PW):
            rows = pl.ds(at, BLOCK_PW)
            result_ref[k, rows, :] = jnp.dot(
                turned_ref[k, rows, :], right, preferred_element_type=F32
            ).astype(BF16)
            copy = pltpu.make_async_copy(
                result_ref.at[k, rows], out_ref.at[k, rows], sem.at[len(copies)]
            )
            copy.start()
            copies.append(copy)
    for copy in copies:
        copy.wait()


def spread_back(core, y, own, other, turned):
    return pl.pallas_call(
        spread_kernel,
        out_shape=jax.ShapeDtypeStruct((2, NPW_DEV, NB_DEV), BF16),
        in_specs=[smem(), smem()] + [vmem()] * 9,
        out_specs=pl.BlockSpec(memory_space=pltpu.HBM),
        scratch_shapes=[
            pltpu.VMEM((2 * NP, NB_DEV), BF16),
            pltpu.VMEM((2, NPW_DEV, NB_DEV), BF16),
            pltpu.SemaphoreType.DMA((2 * NPW_DEV // BLOCK_PW,)),
        ],
        compiler_params=params(16),
        cost_estimate=cost(8 * NP * NPW_DEV * NB_DEV, 6 * MIB),
    )(core, y, *own, *other, turned)


def shards(waves, projectors, coupling, offsets, counts):
    pw, band = lax.axis_index("pw"), lax.axis_index("band")
    core, y, band = (i.reshape(1) for i in (pw & 1, (pw >> 1) & 3, band))

    distant = over_band(projectors, 1)
    near = [over_band(projectors, bits) for bits in (6, 4, 2)] + [projectors]
    far = [over_band(distant, bits) for bits in (6, 4, 2)] + [distant]
    pick = gathered_order(y, band)
    pick, _ = lax.optimization_barrier((pick, distant))
    left, waves = ahead(pick, offsets, counts, coupling, waves)
    sums = project_near(left, waves, near)
    keep, send = project_far(core, sums, left, waves, far)
    turned = turn(near + far)
    total = (keep + over_pw(send, 1).astype(F32)).reshape(4, CHUNK, NB_DEV)

    sums = total[0]
    for arrived in [over_pw(total[s].astype(BF16), 2 * s) for s in (3, 1, 2)]:
        sums = sums + arrived.astype(F32)
    sent = sums.astype(BF16)
    for arrived in [over_pw(sent, 8 * s) for s in (3, 1, 2)]:
        sums = sums + arrived.astype(F32)
    mine = sums.astype(BF16)
    own = [mine] + [over_pw(mine, 2 * s) for s in SLOTS[1:]]
    other = [over_pw(chunk, 1) for chunk in own]
    return spread_back(core, y, own, other, turned)


def solution(mesh):
    placed = (P(None, "pw", "band"), P(None, "band", "pw"), P(), P(), P())
    return jax.shard_map(
        shards, mesh=mesh, in_specs=placed, out_specs=P(None, "pw", "band"), check_vma=False
    )
```

```python
import jax
import jax.numpy as jnp
from jax import lax
from jax.experimental import pallas as pl
from jax.experimental.pallas import tpu as pltpu
from jax.sharding import PartitionSpec as P

NP = 128
NATOM = 12
M = 13
ROWS = 16
HALF = 64
NPW_DEV = 1280
NB_DEV = 896
CHUNK = 32
SLOTS = (0, 2, 3, 1)
BLOCK_PW = 320
BF16 = jnp.bfloat16
F32 = jnp.float32
MIB = 1024 * 1024


def over_pw(x, bits):
    return lax.ppermute(x, "pw", [(i, i ^ bits) for i in range(32)])


def over_band(x, bits):
    return lax.ppermute(x, "band", [(i, i ^ bits) for i in range(8)])


def vmem():
    return pl.BlockSpec(memory_space=pltpu.VMEM)


def smem():
    return pl.BlockSpec(memory_space=pltpu.SMEM)


def params(mib):
    return pltpu.CompilerParams(vmem_limit_bytes=mib * MIB)


def cost(flops, nbytes):
    return pl.CostEstimate(flops=flops, bytes_accessed=nbytes, transcendentals=0)


def two_terms(x):
    high = x.astype(BF16)
    return high, (x - high.astype(F32)).astype(BF16)


def ahead_kernel(
    pick_ref,
    offsets_hbm,
    counts_hbm,
    coupling_hbm,
    waves_hbm,
    left_ref,
    waves_ref,
    placed_ref,
    offsets_ref,
    counts_ref,
    coupling_ref,
    sem,
):
    pairs = (
        (offsets_hbm, offsets_ref),
        (counts_hbm, counts_ref),
        (coupling_hbm, coupling_ref),
        (waves_hbm, waves_ref),
    )
    copies = [pltpu.make_async_copy(a, b, sem.at[i]) for i, (a, b) in enumerate(pairs)]
    for copy in copies:
        copy.start()
    placed_ref[...] = jnp.zeros(placed_ref.shape, F32)
    for copy in copies[:3]:
        copy.wait()
    row = lax.broadcasted_iota(jnp.int32, (M, NP), 0)
    column = lax.broadcasted_iota(jnp.int32, (M, NP), 1)
    for atom in range(NATOM):
        at, count = offsets_ref[atom], counts_ref[atom]
        wide = jnp.concatenate([coupling_ref[atom], jnp.zeros((M, NP - M), F32)], axis=1)
        wide = jnp.where((row < count) & (column < count), wide, 0.0)
        placed_ref[pl.ds(at, M), :] = pltpu.roll(wide, at, 1)
    placed = placed_ref[:NP, :]
    block = (placed + placed.T) * 0.5
    pick, pick_turned = pick_ref[0], pick_ref[1]

    def reorder(part):
        part = jnp.dot(part, pick, preferred_element_type=F32).astype(BF16)
        return jnp.dot(pick_turned, part, preferred_element_type=F32).astype(BF16)

    high, low = (reorder(part) for part in two_terms(block))
    for h in range(2):
        columns = slice(h * HALF, (h + 1) * HALF)
        left_ref[h] = jnp.concatenate(
            [high[:, columns], high[:, columns], low[:, columns]], axis=1
        )
    copies[3].wait()


def pick_kernel(y_ref, band_ref, pick_ref):
    def pick(place):
        piece = place >> 4
        piece = ((piece & 3) << 1) | (piece >> 2)
        number = (jnp.bitwise_xor(piece, band_ref[0]) << 4) | (place & 15)
        projector = lax.broadcasted_iota(jnp.int32, (NP, NP), 0)
        return (projector == number).astype(F32)

    place = lax.broadcasted_iota(jnp.int32, (NP, NP), 1)
    pick_ref[0] = pick(place).astype(BF16)
    pick_ref[1] = pick(jnp.bitwise_xor(place, y_ref[0] << 5)).T.astype(BF16)


def gathered_order(y, band):
    return pl.pallas_call(
        pick_kernel,
        out_shape=jax.ShapeDtypeStruct((2, NP, NP), BF16),
        in_specs=[smem(), smem()],
        out_specs=vmem(),
        compiler_params=params(8),
        cost_estimate=cost(4 * 10**9, 1),
    )(y, band)


def ahead(pick, offsets, counts, coupling, waves):
    hbm = pl.BlockSpec(memory_space=pltpu.HBM)
    return pl.pallas_call(
        ahead_kernel,
        out_shape=(
            jax.ShapeDtypeStruct((2, NP, 3 * HALF), BF16),
            jax.ShapeDtypeStruct(waves.shape, BF16),
        ),
        in_specs=[vmem()] + [hbm] * 4,
        out_specs=(vmem(), vmem()),
        scratch_shapes=[
            pltpu.VMEM((NP + ROWS, NP), F32),
            pltpu.SMEM((NATOM,), jnp.int32),
            pltpu.SMEM((NATOM,), jnp.int32),
            pltpu.VMEM((NATOM, M, M), F32),
            pltpu.SemaphoreType.DMA((4,)),
        ],
        compiler_params=params(46),
        cost_estimate=cost(2 * 10**9, 8 * MIB),
    )(pick, offsets, counts, coupling, waves)


def coupled_parts(h, pieces, left_ref, waves_ref, rows_ref):
    for i, piece in enumerate(pieces):
        at = (3 - i) * ROWS
        rows_ref[pl.ds(at, ROWS), :] = piece[0]
        rows_ref[pl.ds(HALF + at, ROWS), :] = piece[1]
    rows = rows_ref[...]
    first = jnp.dot(rows, waves_ref[0], preferred_element_type=F32)
    second = jnp.dot(rows, waves_ref[1], preferred_element_type=F32)
    left = left_ref[h]

    def couple(part):
        high, low = two_terms(part)
        right = jnp.concatenate([high, low, high], axis=0)
        return jnp.dot(left, right, preferred_element_type=F32)

    return couple(first[:HALF] + second[HALF:]), couple(second[:HALF] - first[HALF:])


def near_kernel(left_ref, waves_ref, *refs):
    pieces, (out_ref, rows_ref) = refs[:4], refs[4:]
    out_ref[0], out_ref[1] = coupled_parts(0, pieces, left_ref, waves_ref, rows_ref)


def project_near(left, waves, pieces):
    return pl.pallas_call(
        near_kernel,
        out_shape=jax.ShapeDtypeStruct((2, NP, NB_DEV), F32),
        in_specs=[vmem()] * 6,
        out_specs=vmem(),
        scratch_shapes=[pltpu.VMEM((NP, NPW_DEV), BF16)],
        compiler_params=params(16),
        cost_estimate=cost(4 * NP * NPW_DEV * NB_DEV, 6 * MIB),
    )(left, waves, *pieces)


def far_kernel(core_ref, near_ref, left_ref, waves_ref, *refs):
    pieces, (keep_ref, send_ref, rows_ref) = refs[:4], refs[4:]

    def sums(out_refs):
        parts = coupled_parts(1, pieces, left_ref, waves_ref, rows_ref)
        for k in range(2):
            out_refs[k][...] = (parts[k] + near_ref[k]).astype(out_refs[k].dtype)

    @pl.when(core_ref[0] == 0)
    def _():
        sums((keep_ref, send_ref))

    @pl.when(core_ref[0] == 1)
    def _():
        sums((send_ref, keep_ref))


def project_far(core, near, left, waves, pieces):
    halves = [jax.ShapeDtypeStruct((NP, NB_DEV), dtype) for dtype in (F32, BF16)]
    return pl.pallas_call(
        far_kernel,
        out_shape=halves,
        in_specs=[smem()] + [vmem()] * 7,
        out_specs=(vmem(), vmem()),
        scratch_shapes=[pltpu.VMEM((NP, NPW_DEV), BF16)],
        compiler_params=params(16),
        cost_estimate=cost(4 * NP * NPW_DEV * NB_DEV, 6 * MIB),
    )(core, near, left, waves, *pieces)


def turn_kernel(*refs):
    pieces, (out_ref, rows_ref) = refs[:8], refs[8:]
    for i, piece in enumerate(pieces):
        at = (i // 4) * HALF + (3 - i % 4) * ROWS
        for k in range(2):
            rows_ref[pl.ds(k * NP + at, ROWS), :] = piece[k]
    turned = rows_ref[...].T
    first, second = turned[:, :NP], turned[:, NP:]
    out_ref[0, :, :NP] = first
    out_ref[0, :, NP:] = -second
    out_ref[1, :, :NP] = second
    out_ref[1, :, NP:] = first


def turn(pieces):
    return pl.pallas_call(
        turn_kernel,
        out_shape=jax.ShapeDtypeStruct((2, NPW_DEV, 2 * NP), BF16),
        in_specs=[vmem()] * 8,
        out_specs=vmem(),
        scratch_shapes=[pltpu.VMEM((2 * NP, NPW_DEV), BF16)],
        compiler_params=params(16),
        cost_estimate=cost(2 * NP * NPW_DEV, 2 * MIB),
    )(*pieces)


def spread_kernel(core_ref, y_ref, *refs):
    own_ref, other_ref = refs[:4], refs[4:8]
    turned_ref, out_ref, right_ref, result_ref, sem = refs[8:]
    core, y = core_ref[0], y_ref[0]
    for s, slot in enumerate(SLOTS):
        at = jnp.bitwise_xor(y, slot) * CHUNK
        half = core if slot % 2 == 0 else 1 - core
        own_at = pl.multiple_of(half * NP + at, CHUNK)
        other_at = pl.multiple_of((1 - half) * NP + at, CHUNK)
        right_ref[pl.ds(own_at, CHUNK), :] = own_ref[s][...]
        right_ref[pl.ds(other_at, CHUNK), :] = other_ref[s][...]
    right = right_ref[...]
    copies = []
    for k in range(2):
        for at in range(0, NPW_DEV, BLOCK_PW):
            rows = pl.ds(at, BLOCK_PW)
            result_ref[k, rows, :] = jnp.dot(
                turned_ref[k, rows, :], right, preferred_element_type=F32
            ).astype(BF16)
            copy = pltpu.make_async_copy(
                result_ref.at[k, rows], out_ref.at[k, rows], sem.at[len(copies)]
            )
            copy.start()
            copies.append(copy)
    for copy in copies:
        copy.wait()


def spread_back(core, y, own, other, turned):
    return pl.pallas_call(
        spread_kernel,
        out_shape=jax.ShapeDtypeStruct((2, NPW_DEV, NB_DEV), BF16),
        in_specs=[smem(), smem()] + [vmem()] * 9,
        out_specs=pl.BlockSpec(memory_space=pltpu.HBM),
        scratch_shapes=[
            pltpu.VMEM((2 * NP, NB_DEV), BF16),
            pltpu.VMEM((2, NPW_DEV, NB_DEV), BF16),
            pltpu.SemaphoreType.DMA((2 * NPW_DEV // BLOCK_PW,)),
        ],
        compiler_params=params(16),
        cost_estimate=cost(8 * NP * NPW_DEV * NB_DEV, 6 * MIB),
    )(core, y, *own, *other, turned)


def shards(waves, projectors, coupling, offsets, counts):
    pw, band = lax.axis_index("pw"), lax.axis_index("band")
    core, y, band = (i.reshape(1) for i in (pw & 1, (pw >> 1) & 3, band))

    distant = over_band(projectors, 1)
    near = [over_band(projectors, bits) for bits in (6, 4, 2)] + [projectors]
    far = [over_band(distant, bits) for bits in (6, 4, 2)] + [distant]
    pick = gathered_order(y, band)
    pick, _ = lax.optimization_barrier((pick, distant))
    left, waves = ahead(pick, offsets, counts, coupling, waves)
    sums = project_near(left, waves, near)
    keep, send = project_far(core, sums, left, waves, far)
    turned = turn(near + far)
    total = (keep + over_pw(send, 1).astype(F32)).reshape(4, CHUNK, NB_DEV)

    sums = total[0]
    for arrived in [over_pw(total[s].astype(BF16), 2 * s) for s in (3, 1, 2)]:
        sums = sums + arrived.astype(F32)
    sent = sums.astype(BF16)
    for arrived in [over_pw(sent, 8 * s) for s in (3, 1, 2)]:
        sums = sums + arrived.astype(F32)
    mine = sums.astype(BF16)
    own = [mine] + [over_pw(mine, 2 * s + s % 2) for s in SLOTS[1:]]
    other = [over_pw(chunk, 1) for chunk in own]
    return spread_back(core, y, own, other, turned)


def solution(mesh):
    placed = (P(None, "pw", "band"), P(None, "band", "pw"), P(), P(), P())
    return jax.shard_map(
        shards, mesh=mesh, in_specs=placed, out_specs=P(None, "pw", "band"), check_vma=False
    )
```

```python
import jax
import jax.numpy as jnp
from jax import lax
from jax.experimental import pallas as pl
from jax.experimental.pallas import tpu as pltpu
from jax.sharding import PartitionSpec as P

NP = 128
NATOM = 12
M = 13
ROWS = 16
HALF = 64
NPW_DEV = 1280
NB_DEV = 896
CHUNK = 32
ORDER = ((3, 2, 1, 0), (2, 3, 1, 0))
SLOTS = (0, 2, 3, 1)
BLOCK_PW = 320
BF16 = jnp.bfloat16
F32 = jnp.float32
MIB = 1024 * 1024


def over_pw(x, bits):
    return lax.ppermute(x, "pw", [(i, i ^ bits) for i in range(32)])


def over_band(x, bits):
    return lax.ppermute(x, "band", [(i, i ^ bits) for i in range(8)])


def vmem():
    return pl.BlockSpec(memory_space=pltpu.VMEM)


def smem():
    return pl.BlockSpec(memory_space=pltpu.SMEM)


def params(mib):
    return pltpu.CompilerParams(vmem_limit_bytes=mib * MIB)


def cost(flops, nbytes):
    return pl.CostEstimate(flops=flops, bytes_accessed=nbytes, transcendentals=0)


def two_terms(x):
    high = x.astype(BF16)
    return high, (x - high.astype(F32)).astype(BF16)


def ahead_kernel(
    pick_ref,
    offsets_hbm,
    counts_hbm,
    coupling_hbm,
    waves_hbm,
    left_ref,
    waves_ref,
    placed_ref,
    offsets_ref,
    counts_ref,
    coupling_ref,
    sem,
):
    pairs = (
        (offsets_hbm, offsets_ref),
        (counts_hbm, counts_ref),
        (coupling_hbm, coupling_ref),
        (waves_hbm, waves_ref),
    )
    copies = [pltpu.make_async_copy(a, b, sem.at[i]) for i, (a, b) in enumerate(pairs)]
    for copy in copies:
        copy.start()
    placed_ref[...] = jnp.zeros(placed_ref.shape, F32)
    for copy in copies[:3]:
        copy.wait()
    row = lax.broadcasted_iota(jnp.int32, (M, NP), 0)
    column = lax.broadcasted_iota(jnp.int32, (M, NP), 1)
    for atom in range(NATOM):
        at, count = offsets_ref[atom], counts_ref[atom]
        wide = jnp.concatenate([coupling_ref[atom], jnp.zeros((M, NP - M), F32)], axis=1)
        wide = jnp.where((row < count) & (column < count), wide, 0.0)
        placed_ref[pl.ds(at, M), :] = pltpu.roll(wide, at, 1)
    placed = placed_ref[:NP, :]
    block = (placed + placed.T) * 0.5
    pick, pick_turned = pick_ref[0], pick_ref[1]

    def reorder(part):
        part = jnp.dot(part, pick, preferred_element_type=F32).astype(BF16)
        return jnp.dot(pick_turned, part, preferred_element_type=F32).astype(BF16)

    high, low = (reorder(part) for part in two_terms(block))
    for h in range(2):
        columns = slice(h * HALF, (h + 1) * HALF)
        left_ref[h] = jnp.concatenate(
            [high[:, columns], high[:, columns], low[:, columns]], axis=1
        )
    copies[3].wait()


def pick_kernel(y_ref, band_ref, pick_ref):
    def pick(place):
        piece = place >> 4
        piece = ((piece & 3) << 1) | (piece >> 2)
        number = (jnp.bitwise_xor(piece, band_ref[0]) << 4) | (place & 15)
        projector = lax.broadcasted_iota(jnp.int32, (NP, NP), 0)
        return (projector == number).astype(F32)

    place = lax.broadcasted_iota(jnp.int32, (NP, NP), 1)
    pick_ref[0] = pick(place).astype(BF16)
    pick_ref[1] = pick(jnp.bitwise_xor(place, y_ref[0] << 5)).T.astype(BF16)


def gathered_order(y, band):
    return pl.pallas_call(
        pick_kernel,
        out_shape=jax.ShapeDtypeStruct((2, NP, NP), BF16),
        in_specs=[smem(), smem()],
        out_specs=vmem(),
        compiler_params=params(8),
        cost_estimate=cost(4 * 10**9, 1),
    )(y, band)


def ahead(pick, offsets, counts, coupling, waves):
    hbm = pl.BlockSpec(memory_space=pltpu.HBM)
    return pl.pallas_call(
        ahead_kernel,
        out_shape=(
            jax.ShapeDtypeStruct((2, NP, 3 * HALF), BF16),
            jax.ShapeDtypeStruct(waves.shape, BF16),
        ),
        in_specs=[vmem()] + [hbm] * 4,
        out_specs=(vmem(), vmem()),
        scratch_shapes=[
            pltpu.VMEM((NP + ROWS, NP), F32),
            pltpu.SMEM((NATOM,), jnp.int32),
            pltpu.SMEM((NATOM,), jnp.int32),
            pltpu.VMEM((NATOM, M, M), F32),
            pltpu.SemaphoreType.DMA((4,)),
        ],
        compiler_params=params(46),
        cost_estimate=cost(2 * 10**9, 8 * MIB),
    )(pick, offsets, counts, coupling, waves)


def coupled_parts(h, pieces, left_ref, waves_ref, rows_ref):
    for i, piece in enumerate(pieces):
        at = ORDER[h][i] * ROWS
        rows_ref[pl.ds(at, ROWS), :] = piece[0]
        rows_ref[pl.ds(HALF + at, ROWS), :] = piece[1]
    rows = rows_ref[...]
    first = jnp.dot(rows, waves_ref[0], preferred_element_type=F32)
    second = jnp.dot(rows, waves_ref[1], preferred_element_type=F32)
    left = left_ref[h]

    def couple(part):
        high, low = two_terms(part)
        right = jnp.concatenate([high, low, high], axis=0)
        return jnp.dot(left, right, preferred_element_type=F32)

    return couple(first[:HALF] + second[HALF:]), couple(second[:HALF] - first[HALF:])


def near_kernel(left_ref, waves_ref, *refs):
    pieces, (out_ref, rows_ref) = refs[:4], refs[4:]
    out_ref[0], out_ref[1] = coupled_parts(0, pieces, left_ref, waves_ref, rows_ref)


def project_near(left, waves, pieces):
    return pl.pallas_call(
        near_kernel,
        out_shape=jax.ShapeDtypeStruct((2, NP, NB_DEV), F32),
        in_specs=[vmem()] * 6,
        out_specs=vmem(),
        scratch_shapes=[pltpu.VMEM((NP, NPW_DEV), BF16)],
        compiler_params=params(16),
        cost_estimate=cost(4 * NP * NPW_DEV * NB_DEV, 6 * MIB),
    )(left, waves, *pieces)


def far_kernel(core_ref, near_ref, left_ref, waves_ref, *refs):
    pieces, (keep_ref, send_ref, rows_ref) = refs[:4], refs[4:]

    def sums(out_refs):
        parts = coupled_parts(1, pieces, left_ref, waves_ref, rows_ref)
        for k in range(2):
            out_refs[k][...] = (parts[k] + near_ref[k]).astype(out_refs[k].dtype)

    @pl.when(core_ref[0] == 0)
    def _():
        sums((keep_ref, send_ref))

    @pl.when(core_ref[0] == 1)
    def _():
        sums((send_ref, keep_ref))


def project_far(core, near, left, waves, pieces):
    halves = [jax.ShapeDtypeStruct((NP, NB_DEV), dtype) for dtype in (F32, BF16)]
    return pl.pallas_call(
        far_kernel,
        out_shape=halves,
        in_specs=[smem()] + [vmem()] * 7,
        out_specs=(vmem(), vmem()),
        scratch_shapes=[pltpu.VMEM((NP, NPW_DEV), BF16)],
        compiler_params=params(16),
        cost_estimate=cost(4 * NP * NPW_DEV * NB_DEV, 6 * MIB),
    )(core, near, left, waves, *pieces)


def turn_kernel(*refs):
    pieces, (out_ref, rows_ref) = refs[:8], refs[8:]
    for i, piece in enumerate(pieces):
        at = (i // 4) * HALF + ORDER[i // 4][i % 4] * ROWS
        for k in range(2):
            rows_ref[pl.ds(k * NP + at, ROWS), :] = piece[k]
    turned = rows_ref[...].T
    first, second = turned[:, :NP], turned[:, NP:]
    out_ref[0, :, :NP] = first
    out_ref[0, :, NP:] = -second
    out_ref[1, :, :NP] = second
    out_ref[1, :, NP:] = first


def turn(pieces):
    return pl.pallas_call(
        turn_kernel,
        out_shape=jax.ShapeDtypeStruct((2, NPW_DEV, 2 * NP), BF16),
        in_specs=[vmem()] * 8,
        out_specs=vmem(),
        scratch_shapes=[pltpu.VMEM((2 * NP, NPW_DEV), BF16)],
        compiler_params=params(16),
        cost_estimate=cost(2 * NP * NPW_DEV, 2 * MIB),
    )(*pieces)


def spread_kernel(core_ref, y_ref, *refs):
    own_ref, other_ref = refs[:4], refs[4:8]
    turned_ref, out_ref, right_ref, result_ref, sem = refs[8:]
    core, y = core_ref[0], y_ref[0]
    for s, slot in enumerate(SLOTS):
        at = jnp.bitwise_xor(y, slot) * CHUNK
        half = core if slot == 0 else 1 - core
        own_at = pl.multiple_of(half * NP + at, CHUNK)
        other_at = pl.multiple_of((1 - half) * NP + at, CHUNK)
        right_ref[pl.ds(own_at, CHUNK), :] = own_ref[s][...]
        right_ref[pl.ds(other_at, CHUNK), :] = other_ref[s][...]
    right = right_ref[...]
    copies = []
    for k in range(2):
        for at in range(0, NPW_DEV, BLOCK_PW):
            rows = pl.ds(at, BLOCK_PW)
            result_ref[k, rows, :] = jnp.dot(
                turned_ref[k, rows, :], right, preferred_element_type=F32
            ).astype(BF16)
            copy = pltpu.make_async_copy(
                result_ref.at[k, rows], out_ref.at[k, rows], sem.at[len(copies)]
            )
            copy.start()
            copies.append(copy)
    for copy in copies:
        copy.wait()


def spread_back(core, y, own, other, turned):
    return pl.pallas_call(
        spread_kernel,
        out_shape=jax.ShapeDtypeStruct((2, NPW_DEV, NB_DEV), BF16),
        in_specs=[smem(), smem()] + [vmem()] * 9,
        out_specs=pl.BlockSpec(memory_space=pltpu.HBM),
        scratch_shapes=[
            pltpu.VMEM((2 * NP, NB_DEV), BF16),
            pltpu.VMEM((2, NPW_DEV, NB_DEV), BF16),
            pltpu.SemaphoreType.DMA((2 * NPW_DEV // BLOCK_PW,)),
        ],
        compiler_params=params(16),
        cost_estimate=cost(8 * NP * NPW_DEV * NB_DEV, 6 * MIB),
    )(core, y, *own, *other, turned)


def shards(waves, projectors, coupling, offsets, counts):
    pw, band = lax.axis_index("pw"), lax.axis_index("band")
    core, y, band = (i.reshape(1) for i in (pw & 1, (pw >> 1) & 3, band))

    distant = over_band(projectors, 1)
    near = [over_band(projectors, bits) for bits in (6, 4, 2)] + [projectors]
    far = [over_band(distant, bits) for bits in (4, 6, 2)] + [distant]
    pick = gathered_order(y, band)
    pick, _ = lax.optimization_barrier((pick, distant))
    left, waves = ahead(pick, offsets, counts, coupling, waves)
    sums = project_near(left, waves, near)
    keep, send = project_far(core, sums, left, waves, far)
    turned = turn(near + far)
    total = (keep + over_pw(send, 1).astype(F32)).reshape(4, CHUNK, NB_DEV)

    sums = total[0]
    for arrived in [over_pw(total[s].astype(BF16), 2 * s) for s in (3, 1, 2)]:
        sums = sums + arrived.astype(F32)
    sent = sums.astype(BF16)
    for arrived in [over_pw(sent, 8 * s) for s in (3, 1, 2)]:
        sums = sums + arrived.astype(F32)
    mine = sums.astype(BF16)
    own = [mine] + [over_pw(mine, 2 * s + 1) for s in SLOTS[1:]]
    other = [over_pw(chunk, 1) for chunk in own]
    return spread_back(core, y, own, other, turned)


def solution(mesh):
    placed = (P(None, "pw", "band"), P(None, "band", "pw"), P(), P(), P())
    return jax.shard_map(
        shards, mesh=mesh, in_specs=placed, out_specs=P(None, "pw", "band"), check_vma=False
    )
```

```python
import jax
import jax.numpy as jnp
from jax import lax
from jax.experimental import pallas as pl
from jax.experimental.pallas import tpu as pltpu
from jax.sharding import PartitionSpec as P

NP = 128
NATOM = 12
M = 13
ROWS = 16
HALF = 64
NPW_DEV = 1280
NB_DEV = 896
CHUNK = 32
ORDER = ((3, 2, 1, 0), (2, 3, 1, 0))
SLOTS = (0, 2, 3, 1)
BLOCK_PW = 320
BF16 = jnp.bfloat16
F32 = jnp.float32
MIB = 1024 * 1024


def over_pw(x, bits):
    return lax.ppermute(x, "pw", [(i, i ^ bits) for i in range(32)])


def over_band(x, bits):
    return lax.ppermute(x, "band", [(i, i ^ bits) for i in range(8)])


def vmem():
    return pl.BlockSpec(memory_space=pltpu.VMEM)


def smem():
    return pl.BlockSpec(memory_space=pltpu.SMEM)


def params(mib):
    return pltpu.CompilerParams(vmem_limit_bytes=mib * MIB)


def cost(flops, nbytes):
    return pl.CostEstimate(flops=flops, bytes_accessed=nbytes, transcendentals=0)


def two_terms(x):
    high = x.astype(BF16)
    return high, (x - high.astype(F32)).astype(BF16)


def ahead_kernel(
    pick_ref,
    offsets_hbm,
    counts_hbm,
    coupling_hbm,
    waves_hbm,
    *refs,
):
    pieces = refs[:4]
    left_ref, waves_ref, near_ref = refs[4:7]
    placed_ref, offsets_ref, counts_ref, coupling_ref, rows_ref, sem = refs[7:]
    pairs = (
        (offsets_hbm, offsets_ref),
        (counts_hbm, counts_ref),
        (coupling_hbm, coupling_ref),
        (waves_hbm.at[0], waves_ref.at[0]),
        (waves_hbm.at[1], waves_ref.at[1]),
    )
    copies = [pltpu.make_async_copy(a, b, sem.at[i]) for i, (a, b) in enumerate(pairs)]
    for copy in copies:
        copy.start()
    placed_ref[...] = jnp.zeros(placed_ref.shape, F32)
    for copy in copies[:3]:
        copy.wait()
    row = lax.broadcasted_iota(jnp.int32, (M, NP), 0)
    column = lax.broadcasted_iota(jnp.int32, (M, NP), 1)
    for atom in range(NATOM):
        at, count = offsets_ref[atom], counts_ref[atom]
        wide = jnp.concatenate([coupling_ref[atom], jnp.zeros((M, NP - M), F32)], axis=1)
        wide = jnp.where((row < count) & (column < count), wide, 0.0)
        placed_ref[pl.ds(at, M), :] = pltpu.roll(wide, at, 1)
    placed = placed_ref[:NP, :]
    block = (placed + placed.T) * 0.5
    pick, pick_turned = pick_ref[0], pick_ref[1]

    def reorder(part):
        part = jnp.dot(part, pick, preferred_element_type=F32).astype(BF16)
        return jnp.dot(pick_turned, part, preferred_element_type=F32).astype(BF16)

    high, low = (reorder(part) for part in two_terms(block))
    for h in range(2):
        columns = slice(h * HALF, (h + 1) * HALF)
        left_ref[h] = jnp.concatenate(
            [high[:, columns], high[:, columns], low[:, columns]], axis=1
        )
    near_ref[0], near_ref[1] = coupled_parts(
        0, pieces, left_ref, waves_ref, rows_ref, copies[3:]
    )


def pick_kernel(y_ref, band_ref, pick_ref):
    def pick(place):
        piece = place >> 4
        piece = ((piece & 3) << 1) | (piece >> 2)
        number = (jnp.bitwise_xor(piece, band_ref[0]) << 4) | (place & 15)
        projector = lax.broadcasted_iota(jnp.int32, (NP, NP), 0)
        return (projector == number).astype(F32)

    place = lax.broadcasted_iota(jnp.int32, (NP, NP), 1)
    pick_ref[0] = pick(place).astype(BF16)
    pick_ref[1] = pick(jnp.bitwise_xor(place, y_ref[0] << 5)).T.astype(BF16)


def gathered_order(y, band):
    return pl.pallas_call(
        pick_kernel,
        out_shape=jax.ShapeDtypeStruct((2, NP, NP), BF16),
        in_specs=[smem(), smem()],
        out_specs=vmem(),
        compiler_params=params(8),
        cost_estimate=cost(4 * 10**9, 1),
    )(y, band)


def ahead(pick, offsets, counts, coupling, waves, pieces):
    hbm = pl.BlockSpec(memory_space=pltpu.HBM)
    return pl.pallas_call(
        ahead_kernel,
        out_shape=(
            jax.ShapeDtypeStruct((2, NP, 3 * HALF), BF16),
            jax.ShapeDtypeStruct(waves.shape, BF16),
            jax.ShapeDtypeStruct((2, NP, NB_DEV), F32),
        ),
        in_specs=[vmem()] + [hbm] * 4 + [vmem()] * 4,
        out_specs=(vmem(), vmem(), vmem()),
        scratch_shapes=[
            pltpu.VMEM((NP + ROWS, NP), F32),
            pltpu.SMEM((NATOM,), jnp.int32),
            pltpu.SMEM((NATOM,), jnp.int32),
            pltpu.VMEM((NATOM, M, M), F32),
            pltpu.VMEM((NP, NPW_DEV), BF16),
            pltpu.SemaphoreType.DMA((5,)),
        ],
        compiler_params=params(46),
        cost_estimate=cost(2 * 10**9, 8 * MIB),
    )(pick, offsets, counts, coupling, waves, *pieces)


def coupled_parts(h, pieces, left_ref, waves_ref, rows_ref, copies=()):
    for i, piece in enumerate(pieces):
        at = ORDER[h][i] * ROWS
        rows_ref[pl.ds(at, ROWS), :] = piece[0]
        rows_ref[pl.ds(HALF + at, ROWS), :] = piece[1]
    rows = rows_ref[...]
    for copy in copies[:1]:
        copy.wait()
    first = jnp.dot(rows, waves_ref[0], preferred_element_type=F32)
    for copy in copies[1:]:
        copy.wait()
    second = jnp.dot(rows, waves_ref[1], preferred_element_type=F32)
    left = left_ref[h]

    def couple(part):
        high, low = two_terms(part)
        right = jnp.concatenate([high, low, high], axis=0)
        return jnp.dot(left, right, preferred_element_type=F32)

    return couple(first[:HALF] + second[HALF:]), couple(second[:HALF] - first[HALF:])


def far_kernel(core_ref, near_ref, left_ref, waves_ref, *refs):
    pieces, (keep_ref, send_ref, rows_ref) = refs[:4], refs[4:]

    def sums(out_refs):
        parts = coupled_parts(1, pieces, left_ref, waves_ref, rows_ref)
        for k in range(2):
            out_refs[k][...] = (parts[k] + near_ref[k]).astype(out_refs[k].dtype)

    @pl.when(core_ref[0] == 0)
    def _():
        sums((keep_ref, send_ref))

    @pl.when(core_ref[0] == 1)
    def _():
        sums((send_ref, keep_ref))


def project_far(core, near, left, waves, pieces):
    halves = [jax.ShapeDtypeStruct((NP, NB_DEV), dtype) for dtype in (F32, BF16)]
    return pl.pallas_call(
        far_kernel,
        out_shape=halves,
        in_specs=[smem()] + [vmem()] * 7,
        out_specs=(vmem(), vmem()),
        scratch_shapes=[pltpu.VMEM((NP, NPW_DEV), BF16)],
        compiler_params=params(16),
        cost_estimate=cost(4 * NP * NPW_DEV * NB_DEV, 6 * MIB),
    )(core, near, left, waves, *pieces)


def turn_kernel(*refs):
    pieces, (out_ref, rows_ref) = refs[:8], refs[8:]
    for i, piece in enumerate(pieces):
        at = (i // 4) * HALF + ORDER[i // 4][i % 4] * ROWS
        for k in range(2):
            rows_ref[pl.ds(k * NP + at, ROWS), :] = piece[k]
    turned = rows_ref[...].T
    first, second = turned[:, :NP], turned[:, NP:]
    out_ref[0, :, :NP] = first
    out_ref[0, :, NP:] = -second
    out_ref[1, :, :NP] = second
    out_ref[1, :, NP:] = first


def turn(pieces):
    return pl.pallas_call(
        turn_kernel,
        out_shape=jax.ShapeDtypeStruct((2, NPW_DEV, 2 * NP), BF16),
        in_specs=[vmem()] * 8,
        out_specs=vmem(),
        scratch_shapes=[pltpu.VMEM((2 * NP, NPW_DEV), BF16)],
        compiler_params=params(16),
        cost_estimate=cost(2 * NP * NPW_DEV, 2 * MIB),
    )(*pieces)


def spread_kernel(core_ref, y_ref, *refs):
    own_ref, other_ref = refs[:4], refs[4:8]
    turned_ref, out_ref, right_ref, result_ref, sem = refs[8:]
    core, y = core_ref[0], y_ref[0]
    for s, slot in enumerate(SLOTS):
        at = jnp.bitwise_xor(y, slot) * CHUNK
        half = core if slot == 0 else 1 - core
        own_at = pl.multiple_of(half * NP + at, CHUNK)
        other_at = pl.multiple_of((1 - half) * NP + at, CHUNK)
        right_ref[pl.ds(own_at, CHUNK), :] = own_ref[s][...]
        right_ref[pl.ds(other_at, CHUNK), :] = other_ref[s][...]
    right = right_ref[...]
    copies = []
    for k in range(2):
        for at in range(0, NPW_DEV, BLOCK_PW):
            rows = pl.ds(at, BLOCK_PW)
            result_ref[k, rows, :] = jnp.dot(
                turned_ref[k, rows, :], right, preferred_element_type=F32
            ).astype(BF16)
            copy = pltpu.make_async_copy(
                result_ref.at[k, rows], out_ref.at[k, rows], sem.at[len(copies)]
            )
            copy.start()
            copies.append(copy)
    for copy in copies:
        copy.wait()


def spread_back(core, y, own, other, turned):
    return pl.pallas_call(
        spread_kernel,
        out_shape=jax.ShapeDtypeStruct((2, NPW_DEV, NB_DEV), BF16),
        in_specs=[smem(), smem()] + [vmem()] * 9,
        out_specs=pl.BlockSpec(memory_space=pltpu.HBM),
        scratch_shapes=[
            pltpu.VMEM((2 * NP, NB_DEV), BF16),
            pltpu.VMEM((2, NPW_DEV, NB_DEV), BF16),
            pltpu.SemaphoreType.DMA((2 * NPW_DEV // BLOCK_PW,)),
        ],
        compiler_params=params(16),
        cost_estimate=cost(8 * NP * NPW_DEV * NB_DEV, 6 * MIB),
    )(core, y, *own, *other, turned)


def shards(waves, projectors, coupling, offsets, counts):
    pw, band = lax.axis_index("pw"), lax.axis_index("band")
    core, y, band = (i.reshape(1) for i in (pw & 1, (pw >> 1) & 3, band))

    distant = over_band(projectors, 1)
    near = [over_band(projectors, bits) for bits in (6, 4, 2)] + [projectors]
    far = [over_band(distant, bits) for bits in (4, 6, 2)] + [distant]
    pick = gathered_order(y, band)
    pick, _ = lax.optimization_barrier((pick, distant))
    left, waves, sums = ahead(pick, offsets, counts, coupling, waves, near)
    keep, send = project_far(core, sums, left, waves, far)
    turned = turn(near + far)
    total = (keep + over_pw(send, 1).astype(F32)).reshape(4, CHUNK, NB_DEV)

    sums = total[0]
    for arrived in [over_pw(total[s].astype(BF16), 2 * s) for s in (3, 1, 2)]:
        sums = sums + arrived.astype(F32)
    sent = sums.astype(BF16)
    for arrived in [over_pw(sent, 8 * s) for s in (3, 1, 2)]:
        sums = sums + arrived.astype(F32)
    mine = sums.astype(BF16)
    own = [mine] + [over_pw(mine, 2 * s + 1) for s in SLOTS[1:]]
    other = [over_pw(chunk, 1) for chunk in own]
    return spread_back(core, y, own, other, turned)


def solution(mesh):
    placed = (P(None, "pw", "band"), P(None, "band", "pw"), P(), P(), P())
    return jax.shard_map(
        shards, mesh=mesh, in_specs=placed, out_specs=P(None, "pw", "band"), check_vma=False
    )
```

```python
import jax
import jax.numpy as jnp
from jax import lax
from jax.experimental import pallas as pl
from jax.experimental.pallas import tpu as pltpu
from jax.sharding import PartitionSpec as P

NP = 128
NATOM = 12
M = 13
ROWS = 16
HALF = 64
NPW_DEV = 1280
NB_DEV = 896
CHUNK = 32
ORDER = ((3, 2, 1, 0), (2, 3, 1, 0))
SLOTS = (0, 2, 3, 1)
BLOCK_PW = 256
BF16 = jnp.bfloat16
F32 = jnp.float32
MIB = 1024 * 1024


def over_pw(x, bits):
    return lax.ppermute(x, "pw", [(i, i ^ bits) for i in range(32)])


def over_band(x, bits):
    return lax.ppermute(x, "band", [(i, i ^ bits) for i in range(8)])


def vmem():
    return pl.BlockSpec(memory_space=pltpu.VMEM)


def smem():
    return pl.BlockSpec(memory_space=pltpu.SMEM)


def params(mib):
    return pltpu.CompilerParams(vmem_limit_bytes=mib * MIB)


def cost(flops, nbytes):
    return pl.CostEstimate(flops=flops, bytes_accessed=nbytes, transcendentals=0)


def two_terms(x):
    high = x.astype(BF16)
    return high, (x - high.astype(F32)).astype(BF16)


def ahead_kernel(
    pick_ref,
    offsets_hbm,
    counts_hbm,
    coupling_hbm,
    waves_hbm,
    left_ref,
    waves_ref,
    placed_ref,
    offsets_ref,
    counts_ref,
    coupling_ref,
    sem,
):
    pairs = (
        (offsets_hbm, offsets_ref),
        (counts_hbm, counts_ref),
        (coupling_hbm, coupling_ref),
        (waves_hbm, waves_ref),
    )
    copies = [pltpu.make_async_copy(a, b, sem.at[i]) for i, (a, b) in enumerate(pairs)]
    for copy in copies:
        copy.start()
    placed_ref[...] = jnp.zeros(placed_ref.shape, F32)
    for copy in copies[:3]:
        copy.wait()
    row = lax.broadcasted_iota(jnp.int32, (M, NP), 0)
    column = lax.broadcasted_iota(jnp.int32, (M, NP), 1)
    for atom in range(NATOM):
        at, count = offsets_ref[atom], counts_ref[atom]
        wide = jnp.concatenate([coupling_ref[atom], jnp.zeros((M, NP - M), F32)], axis=1)
        wide = jnp.where((row < count) & (column < count), wide, 0.0)
        placed_ref[pl.ds(at, M), :] = pltpu.roll(wide, at, 1)
    placed = placed_ref[:NP, :]
    block = (placed + placed.T) * 0.5
    pick, pick_turned = pick_ref[0], pick_ref[1]

    def reorder(part):
        part = jnp.dot(part, pick, preferred_element_type=F32).astype(BF16)
        return jnp.dot(pick_turned, part, preferred_element_type=F32).astype(BF16)

    high, low = (reorder(part) for part in two_terms(block))
    for h in range(2):
        columns = slice(h * HALF, (h + 1) * HALF)
        left_ref[h] = jnp.concatenate(
            [high[:, columns], high[:, columns], low[:, columns]], axis=1
        )
    copies[3].wait()


def pick_kernel(y_ref, band_ref, pick_ref):
    def pick(place):
        piece = place >> 4
        piece = ((piece & 3) << 1) | (piece >> 2)
        number = (jnp.bitwise_xor(piece, band_ref[0]) << 4) | (place & 15)
        projector = lax.broadcasted_iota(jnp.int32, (NP, NP), 0)
        return (projector == number).astype(F32)

    place = lax.broadcasted_iota(jnp.int32, (NP, NP), 1)
    pick_ref[0] = pick(place).astype(BF16)
    pick_ref[1] = pick(jnp.bitwise_xor(place, y_ref[0] << 5)).T.astype(BF16)


def gathered_order(y, band):
    return pl.pallas_call(
        pick_kernel,
        out_shape=jax.ShapeDtypeStruct((2, NP, NP), BF16),
        in_specs=[smem(), smem()],
        out_specs=vmem(),
        compiler_params=params(8),
        cost_estimate=cost(4 * 10**9, 1),
    )(y, band)


def ahead(pick, offsets, counts, coupling, waves):
    hbm = pl.BlockSpec(memory_space=pltpu.HBM)
    return pl.pallas_call(
        ahead_kernel,
        out_shape=(
            jax.ShapeDtypeStruct((2, NP, 3 * HALF), BF16),
            jax.ShapeDtypeStruct(waves.shape, BF16),
        ),
        in_specs=[vmem()] + [hbm] * 4,
        out_specs=(vmem(), vmem()),
        scratch_shapes=[
            pltpu.VMEM((NP + ROWS, NP), F32),
            pltpu.SMEM((NATOM,), jnp.int32),
            pltpu.SMEM((NATOM,), jnp.int32),
            pltpu.VMEM((NATOM, M, M), F32),
            pltpu.SemaphoreType.DMA((4,)),
        ],
        compiler_params=params(46),
        cost_estimate=cost(2 * 10**9, 8 * MIB),
    )(pick, offsets, counts, coupling, waves)


def coupled_parts(h, pieces, left_ref, waves_ref, rows_ref):
    for i, piece in enumerate(pieces):
        at = ORDER[h][i] * ROWS
        rows_ref[pl.ds(at, ROWS), :] = piece[0]
        rows_ref[pl.ds(HALF + at, ROWS), :] = piece[1]
    rows = rows_ref[...]
    first = jnp.dot(rows, waves_ref[0], preferred_element_type=F32)
    second = jnp.dot(rows, waves_ref[1], preferred_element_type=F32)
    left = left_ref[h]

    def couple(part):
        high, low = two_terms(part)
        right = jnp.concatenate([high, low, high], axis=0)
        return jnp.dot(left, right, preferred_element_type=F32)

    return couple(first[:HALF] + second[HALF:]), couple(second[:HALF] - first[HALF:])


def near_kernel(left_ref, waves_ref, *refs):
    pieces, (out_ref, rows_ref) = refs[:4], refs[4:]
    out_ref[0], out_ref[1] = coupled_parts(0, pieces, left_ref, waves_ref, rows_ref)


def project_near(left, waves, pieces):
    return pl.pallas_call(
        near_kernel,
        out_shape=jax.ShapeDtypeStruct((2, NP, NB_DEV), F32),
        in_specs=[vmem()] * 6,
        out_specs=vmem(),
        scratch_shapes=[pltpu.VMEM((NP, NPW_DEV), BF16)],
        compiler_params=params(16),
        cost_estimate=cost(4 * NP * NPW_DEV * NB_DEV, 6 * MIB),
    )(left, waves, *pieces)


def far_kernel(core_ref, near_ref, left_ref, waves_ref, *refs):
    pieces, (keep_ref, send_ref, rows_ref) = refs[:4], refs[4:]

    def sums(out_refs):
        parts = coupled_parts(1, pieces, left_ref, waves_ref, rows_ref)
        for k in range(2):
            out_refs[k][...] = (parts[k] + near_ref[k]).astype(out_refs[k].dtype)

    @pl.when(core_ref[0] == 0)
    def _():
        sums((keep_ref, send_ref))

    @pl.when(core_ref[0] == 1)
    def _():
        sums((send_ref, keep_ref))


def project_far(core, near, left, waves, pieces):
    halves = [jax.ShapeDtypeStruct((NP, NB_DEV), dtype) for dtype in (F32, BF16)]
    return pl.pallas_call(
        far_kernel,
        out_shape=halves,
        in_specs=[smem()] + [vmem()] * 7,
        out_specs=(vmem(), vmem()),
        scratch_shapes=[pltpu.VMEM((NP, NPW_DEV), BF16)],
        compiler_params=params(16),
        cost_estimate=cost(4 * NP * NPW_DEV * NB_DEV, 6 * MIB),
    )(core, near, left, waves, *pieces)


def turn_kernel(*refs):
    pieces, (out_ref, rows_ref) = refs[:8], refs[8:]
    for i, piece in enumerate(pieces):
        at = (i // 4) * HALF + ORDER[i // 4][i % 4] * ROWS
        for k in range(2):
            rows_ref[pl.ds(k * NP + at, ROWS), :] = piece[k]
    turned = rows_ref[...].T
    first, second = turned[:, :NP], turned[:, NP:]
    out_ref[0, :, :NP] = first
    out_ref[0, :, NP:] = -second
    out_ref[1, :, :NP] = second
    out_ref[1, :, NP:] = first


def turn(pieces):
    return pl.pallas_call(
        turn_kernel,
        out_shape=jax.ShapeDtypeStruct((2, NPW_DEV, 2 * NP), BF16),
        in_specs=[vmem()] * 8,
        out_specs=vmem(),
        scratch_shapes=[pltpu.VMEM((2 * NP, NPW_DEV), BF16)],
        compiler_params=params(16),
        cost_estimate=cost(2 * NP * NPW_DEV, 2 * MIB),
    )(*pieces)


def spread_kernel(core_ref, y_ref, *refs):
    own_ref, other_ref = refs[:4], refs[4:8]
    turned_ref, out_ref, right_ref, result_ref, sem = refs[8:]
    core, y = core_ref[0], y_ref[0]
    for s, slot in enumerate(SLOTS):
        at = jnp.bitwise_xor(y, slot) * CHUNK
        half = core if slot == 0 else 1 - core
        own_at = pl.multiple_of(half * NP + at, CHUNK)
        other_at = pl.multiple_of((1 - half) * NP + at, CHUNK)
        right_ref[pl.ds(own_at, CHUNK), :] = own_ref[s][...]
        right_ref[pl.ds(other_at, CHUNK), :] = other_ref[s][...]
    right = right_ref[...]
    copies = []
    for k in range(2):
        for at in range(0, NPW_DEV, BLOCK_PW):
            rows = pl.ds(at, BLOCK_PW)
            result_ref[k, rows, :] = jnp.dot(
                turned_ref[k, rows, :], right, preferred_element_type=F32
            ).astype(BF16)
            copy = pltpu.make_async_copy(
                result_ref.at[k, rows], out_ref.at[k, rows], sem.at[len(copies)]
            )
            copy.start()
            copies.append(copy)
    for copy in copies:
        copy.wait()


def spread_back(core, y, own, other, turned):
    return pl.pallas_call(
        spread_kernel,
        out_shape=jax.ShapeDtypeStruct((2, NPW_DEV, NB_DEV), BF16),
        in_specs=[smem(), smem()] + [vmem()] * 9,
        out_specs=pl.BlockSpec(memory_space=pltpu.HBM),
        scratch_shapes=[
            pltpu.VMEM((2 * NP, NB_DEV), BF16),
            pltpu.VMEM((2, NPW_DEV, NB_DEV), BF16),
            pltpu.SemaphoreType.DMA((2 * NPW_DEV // BLOCK_PW,)),
        ],
        compiler_params=params(16),
        cost_estimate=cost(8 * NP * NPW_DEV * NB_DEV, 6 * MIB),
    )(core, y, *own, *other, turned)


def shards(waves, projectors, coupling, offsets, counts):
    pw, band = lax.axis_index("pw"), lax.axis_index("band")
    core, y, band = (i.reshape(1) for i in (pw & 1, (pw >> 1) & 3, band))

    distant = over_band(projectors, 1)
    near = [over_band(projectors, bits) for bits in (6, 4, 2)] + [projectors]
    far = [over_band(distant, bits) for bits in (4, 6, 2)] + [distant]
    pick = gathered_order(y, band)
    pick, _ = lax.optimization_barrier((pick, distant))
    left, waves = ahead(pick, offsets, counts, coupling, waves)
    sums = project_near(left, waves, near)
    keep, send = project_far(core, sums, left, waves, far)
    turned = turn(near + far)
    total = (keep + over_pw(send, 1).astype(F32)).reshape(4, CHUNK, NB_DEV)

    sums = total[0]
    for arrived in [over_pw(total[s].astype(BF16), 2 * s) for s in (3, 1, 2)]:
        sums = sums + arrived.astype(F32)
    sent = sums.astype(BF16)
    for arrived in [over_pw(sent, 8 * s) for s in (3, 1, 2)]:
        sums = sums + arrived.astype(F32)
    mine = sums.astype(BF16)
    own = [mine] + [over_pw(mine, 2 * s + 1) for s in SLOTS[1:]]
    other = [over_pw(chunk, 1) for chunk in own]
    return spread_back(core, y, own, other, turned)


def solution(mesh):
    placed = (P(None, "pw", "band"), P(None, "band", "pw"), P(), P(), P())
    return jax.shard_map(
        shards, mesh=mesh, in_specs=placed, out_specs=P(None, "pw", "band"), check_vma=False
    )
```
